32 devices in a mesh: groups: 2 (over y), rows: 16 (over z, x, core).
Axes of the slice: x: 2, y: 2, z: 4, core: 2. Of those that a mesh axis runs over, the one named last changes fastest.
Arguments:
- grad: bfloat16 [12288, 2880], P(('groups', 'rows')), parts along dimension 0, may hold values from -40 to 40
- moment: bfloat16 [12288, 2880], P(('groups', 'rows')), parts along dimension 0, may hold values from -6 to 6
- second: float32 [12288, 64], P(('groups', 'rows')), parts along dimension 0, may hold values from 0.05 to 2
- basis: bfloat16 [128, 2880], P(('groups', 'rows')), parts along dimension 0, may hold values from -0.109375 to 0.109375
Outputs:
- update: bfloat16 [12288, 2880], P(('groups', 'rows')), parts along dimension 0
- moment_next: bfloat16 [12288, 2880], P(('groups', 'rows')), parts along dimension 0
- second_next: float32 [12288, 64], P(('groups', 'rows')), parts along dimension 0
- basis_next: float32 [128, 2880], P(('groups', 'rows')), parts along dimension 0
The draws below stay inside these ranges and needn't reach their ends.
There are 2 independent parts, one for each index of `groups`. The reference program is written for one: setup_inputs(seed, part) draws one part's arguments, and reference() takes and returns one part's arrays. A program takes and returns all parts, laid end to end along the dimension named above; each array names one. Nothing has to cross between parts.
All inputs are finite; a program needn't handle non-finite values.
Results may differ from the reference program's by a relative error of at most 0.0065.
Values may be sent and summed in bfloat16 or wider, within the bound.
No kernel may reach another device: no remote copies, remote signals or barrier semaphores. Data moves between devices by JAX's collectives and lax.ppermute only.
A program may use at most 128 MiB of HBM per device.

```python
import math
import jax
import jax.numpy as jnp
from jax import lax

D = 2880
ROWS = 6144
K = 64


def draw_grad(key, part):
    key = jax.random.fold_in(key, 11)
    first, second_key, third = jax.random.split(key, 3)
    column_scale = jnp.exp(jax.random.uniform(second_key, (1, D), jnp.float32, math.log(0.3), math.log(3.0)))
    base = jnp.clip(jax.random.normal(first, (ROWS, D), jnp.float32), -6.0, 6.0)
    row_scale = jnp.exp(jax.random.uniform(third, (ROWS, 1), jnp.float32, math.log(0.5), math.log(2.0)))
    values = base * row_scale * column_scale
    return values.astype(jnp.bfloat16)


def level_of(stream_key, dims, pieces, low, high):
    level = 1.0
    for position, parts in pieces:
        steps = jax.random.uniform(jax.random.fold_in(jax.random.fold_in(stream_key, 6), position), (parts,), jnp.float32, low / len(pieces), high / len(pieces))
        level = level * jnp.repeat(jnp.exp(steps), dims[position] // parts).reshape((-1,) + (1,) * (len(dims) - 1 - position))
    return level


def normal_values(key, extent, width, most, cuts=(), dtype=jnp.bfloat16):
    entries = jax.random.normal(key, extent, jnp.float32) * width
    if len(cuts) > 0:
        entries = level_of(key, extent, cuts, -0.22, 0.18) * entries
    return jnp.clip(entries, min=-most, max=most).astype(dtype)


def setup_inputs(seed: int = 0, part: int = 0) -> dict:
    splits = jax.random.split(jax.random.key(seed), 5)
    part_keys = jax.random.split(jax.random.fold_in(splits[4], part), 5)
    return {
        "grad": draw_grad(jax.random.fold_in(jax.random.fold_in(splits[4], part), 71), part),
        "moment": normal_values(part_keys[1], (ROWS, D), 1.0, 6.0, ((0, 16),)),
        "second": jnp.clip(jnp.exp(math.log(2.0) - 3.6888794 * jax.random.uniform(part_keys[2], (ROWS, K), jnp.float32) ** level_of(part_keys[2], (ROWS, K), ((0, 16),), -0.2, 0.2)), 0.05, 2.0),
        "basis": normal_values(part_keys[3], (K, D), D ** -0.5, 0.109375, ((0, 16),)),
    }


def reference(grad, moment, second, basis):
    moment_next = (0.9 * moment.astype(jnp.float32) + 0.1 * grad.astype(jnp.float32)).astype(jnp.bfloat16)
    rot_grad = jnp.dot(grad, basis.T, preferred_element_type=jnp.float32)
    rot_moment = jnp.dot(moment_next, basis.T, preferred_element_type=jnp.float32)
    second_next = 0.95 * second + 0.05 * rot_grad * rot_grad
    scaled = (rot_moment / (jnp.sqrt(second_next) + 1e-08)).astype(jnp.bfloat16)
    update = jnp.dot(scaled, basis, preferred_element_type=jnp.float32).astype(jnp.bfloat16)
    rot_rounded = rot_grad.astype(jnp.bfloat16)
    power = jnp.dot(rot_rounded.T, grad, preferred_element_type=jnp.float32)
    basis_next = power / jnp.sqrt(lax.optimization_barrier(jnp.mean(power * power, axis=1, keepdims=True)) + 1e-06)
    return (update, moment_next, second_next, basis_next)
```

```python
import jax
import jax.numpy as jnp
from jax import lax
from jax.sharding import PartitionSpec as P


def shards(n, grad, moment, second, basis):
    bits = n.bit_length() - 1
    me = lax.axis_index("rows")
    own = basis.shape[0]
    rows, depth = grad.shape

    def exchange(value, bit):
        return lax.ppermute(value, "rows", [(i, i ^ (1 << bit)) for i in range(n)])

    def reorder(value):
        value = value.reshape((2,) * bits + (own, rows))
        for bit in range(bits):
            axis = bits - 1 - bit
            value = jnp.where((me >> bit) & 1, jnp.flip(value, axis), value)
        return value

    held = basis
    for bit in reversed(range(bits)):
        held = jnp.concatenate([held, exchange(held, bit)], 0)

    moment_next = (0.9 * moment.astype(jnp.float32) + 0.1 * grad.astype(jnp.float32)).astype(
        jnp.bfloat16
    )
    rot_grad = lax.dot_general(
        held, grad, (((1,), (1,)), ((), ())), preferred_element_type=jnp.float32
    )
    partial = jnp.dot(rot_grad.astype(jnp.bfloat16), grad, preferred_element_type=jnp.float32)
    for bit in range(bits):
        half = partial.shape[0] // 2
        partial = partial[:half] + exchange(partial[half:].astype(jnp.bfloat16), bit).astype(
            jnp.float32
        )
    basis_next = partial / jnp.sqrt(jnp.mean(partial * partial, axis=1, keepdims=True) + 1e-06)

    rot_moment = lax.dot_general(
        held, moment_next, (((1,), (1,)), ((), ())), preferred_element_type=jnp.float32
    )
    turn = tuple(reversed(range(bits))) + (bits, bits + 1)
    mine = reorder(second.T).transpose(turn).reshape(n * own, rows)
    mine = 0.95 * mine + 0.05 * rot_grad * rot_grad
    scaled = (rot_moment / (jnp.sqrt(mine) + 1e-08)).astype(jnp.bfloat16)
    update = lax.dot_general(
        scaled, held, (((0,), (0,)), ((), ())), preferred_element_type=jnp.float32
    ).astype(jnp.bfloat16)
    back = mine.reshape((2,) * bits + (own, rows)).transpose(turn)
    second_next = reorder(back).reshape(n * own, rows).T
    return update, moment_next, second_next, basis_next


def solution(mesh):
    n = mesh.shape["rows"]
    placed = P(("groups", "rows"), None)
    return jax.shard_map(
        lambda *arrays: shards(n, *arrays),
        mesh=mesh,
        in_specs=(placed,) * 4,
        out_specs=(placed,) * 4,
        check_vma=False,
    )
```

```python
import jax
import jax.numpy as jnp
import numpy as np
from jax import lax
from jax.experimental import pallas as pl
from jax.experimental.pallas import tpu as pltpu
from jax.sharding import PartitionSpec as P

PARTS = 3


def moment_kernel(*refs):
    grad, moment, out = refs[0], refs[1], refs[-1]
    out[...] = (0.9 * moment[...].astype(jnp.float32) + 0.1 * grad[...].astype(jnp.float32)).astype(
        jnp.bfloat16
    )


def moment_part(part, grad, moment, after, so_far):
    depth, rows = grad.shape
    steps = 3
    size = depth // (PARTS * steps)
    block = pl.BlockSpec((size, rows), lambda i: (part * steps + i, 0))
    anywhere = pl.BlockSpec(memory_space=pl.ANY)
    extra = (after,) if so_far is None else (after, so_far)
    return pl.pallas_call(
        moment_kernel,
        grid=(steps,),
        in_specs=[block, block] + [anywhere] * len(extra),
        out_specs=block,
        out_shape=jax.ShapeDtypeStruct((depth, rows), jnp.bfloat16),
        input_output_aliases={} if so_far is None else {3: 0},
        cost_estimate=pl.CostEstimate(
            flops=3 * size * steps * rows, bytes_accessed=6 * size * steps * rows, transcendentals=0
        ),
        name="moment",
    )(grad, moment, *extra)


def shards(n, grad, moment, second, basis):
    bits = n.bit_length() - 1
    chip_bits = bits - 1
    me = lax.axis_index("rows")
    own = basis.shape[0]
    rows, depth = grad.shape

    def half_of(i):
        return i.bit_count() & 1

    orders = (
        tuple(reversed(range(chip_bits))),
        (0,) + tuple(reversed(range(1, chip_bits))),
    )

    def exchange(value, step):
        pairs = [(i, i ^ (2 << orders[half_of(i)][step]) ^ 1) for i in range(n)]
        return lax.ppermute(value, "rows", pairs)

    def across(value):
        return lax.ppermute(value, "rows", [(i, i ^ 1) for i in range(n)])

    parity = me
    for shift in (4, 2, 1):
        parity = parity ^ (parity >> shift)
    my_half = parity & 1

    grad_t, moment_t = grad.T, moment.T
    other_grad = across(grad)

    held = basis
    moment_next = None
    for step in range(chip_bits):
        come = exchange(held, step)
        if step < PARTS:
            moment_next = moment_part(step, grad_t, moment_t, held, moment_next)
            come, moment_next = lax.optimization_barrier((come, moment_next))
        held = jnp.concatenate([held, come], 0)
    for step in range(chip_bits, PARTS):
        moment_next = moment_part(step, grad_t, moment_t, held, moment_next)

    def rotate(basis_rows, values):
        return lax.dot_general(
            basis_rows, values, (((1,), (1,)), ((), ())), preferred_element_type=jnp.float32
        )

    rot_own = rotate(held, grad)
    rot_other = rotate(held, other_grad)
    rot_own, rot_other = lax.optimization_barrier((rot_own, rot_other))
    partial = jnp.dot(rot_own.astype(jnp.bfloat16), grad, preferred_element_type=jnp.float32)
    partial += jnp.dot(rot_other.astype(jnp.bfloat16), other_grad, preferred_element_type=jnp.float32)
    held_later, partial = lax.optimization_barrier((held, partial))
    whole = jnp.concatenate([held, across(held_later)], 0)
    rot_grad = jnp.concatenate([rot_own, rotate(whole[rot_own.shape[0] :], grad)], 0)
    rot_moment = lax.dot_general(
        whole, moment_next, (((1,), (0,)), ((), ())), preferred_element_type=jnp.float32
    )

    cube = (2,) * bits + (own, rows)
    odd = np.array([half_of(o) for o in range(n // 2)]).reshape((2,) * chip_bits + (1, 1, 1)) == 1

    def flips(value):
        for bit in range(bits):
            axis = bits - 1 - bit
            value = jnp.where((me >> bit) & 1, jnp.flip(value, axis), value)
        return value

    def swap(value):
        return jnp.where(odd, jnp.flip(value, chip_bits), value)

    turns = tuple(tuple(chip_bits - 1 - b for b in reversed(order)) for order in orders)
    rest = (chip_bits, chip_bits + 1)

    def turned(value, turn, back):
        turn = tuple(np.argsort(turn)) if back else turn
        return value.transpose(turn + rest)

    def by_half(first, back):
        pair = [turned(first, turn, back) for turn in turns]
        return jnp.where(my_half == 0, pair[0], pair[1]), jnp.where(my_half == 0, pair[1], pair[0])

    placed = swap(flips(second.T.reshape(cube)))
    mine = by_half(placed[(slice(None),) * chip_bits + (0,)], False)[0]
    theirs = by_half(placed[(slice(None),) * chip_bits + (1,)], False)[1]
    both = jnp.concatenate([mine.reshape(-1, rows), theirs.reshape(-1, rows)], 0)
    both = 0.95 * both + 0.05 * rot_grad * rot_grad
    scaled = (rot_moment / (jnp.sqrt(both) + 1e-08)).astype(jnp.bfloat16)
    both, scaled = lax.optimization_barrier((both, scaled))
    def shrink(partial, step, *beside):
        half = partial.shape[0] // 2
        come = exchange(partial[half:].astype(jnp.bfloat16), step)
        if beside:
            come, *beside = lax.optimization_barrier((come, *beside))
        return partial[:half] + come.astype(jnp.float32), beside

    partial, (both, scaled) = shrink(partial, chip_bits - 1, both, scaled)
    update = lax.dot_general(
        scaled, whole, (((0,), (0,)), ((), ())), preferred_element_type=jnp.float32
    ).astype(jnp.bfloat16)
    partial, (update,) = shrink(partial, chip_bits - 2, update)
    for step in reversed(range(chip_bits - 2)):
        partial, _ = shrink(partial, step)
    basis_next = partial / jnp.sqrt(jnp.mean(partial * partial, axis=1, keepdims=True) + 1e-06)
    count = rot_own.shape[0]
    half_cube = (2,) * chip_bits + (own, rows)
    mine = by_half(both[:count].reshape(half_cube), True)[0]
    theirs = by_half(both[count:].reshape(half_cube), True)[1]
    back = flips(swap(jnp.stack([mine, theirs], chip_bits)))
    second_next = back.reshape(n * own, rows).T
    return update, moment_next.T, second_next, basis_next


def solution(mesh):
    n = mesh.shape["rows"]
    placed = P(("groups", "rows"), None)
    return jax.shard_map(
        lambda *arrays: shards(n, *arrays),
        mesh=mesh,
        in_specs=(placed,) * 4,
        out_specs=(placed,) * 4,
        check_vma=False,
    )
```

```python
import jax
import jax.numpy as jnp
import numpy as np
from jax import lax
from jax.sharding import PartitionSpec as P

def shards(n, grad, moment, second, basis):
    bits = n.bit_length() - 1
    chip_bits = bits - 1
    me = lax.axis_index("rows")
    own = basis.shape[0]
    rows, depth = grad.shape

    def half_of(i):
        return i.bit_count() & 1

    orders = (
        tuple(reversed(range(chip_bits))),
        (0,) + tuple(reversed(range(1, chip_bits))),
    )

    def exchange(value, step):
        pairs = [(i, i ^ (2 << orders[half_of(i)][step]) ^ 1) for i in range(n)]
        return lax.ppermute(value, "rows", pairs)

    def across(value):
        return lax.ppermute(value, "rows", [(i, i ^ 1) for i in range(n)])

    parity = me
    for shift in (4, 2, 1):
        parity = parity ^ (parity >> shift)
    my_half = parity & 1

    other_grad = across(grad)

    held = basis
    for step in range(chip_bits):
        if step == 2:
            held, moment = lax.optimization_barrier((held, moment))
        come = exchange(held, step)
        if step == 0:
            come, other_grad = lax.optimization_barrier((come, other_grad))
        if step == 2:
            moment_next = (
                0.9 * moment.astype(jnp.float32) + 0.1 * grad.astype(jnp.float32)
            ).astype(jnp.bfloat16)
            come, moment_next = lax.optimization_barrier((come, moment_next))
        held = jnp.concatenate([held, come], 0)

    def rotate(basis_rows, values):
        return lax.dot_general(
            basis_rows, values, (((1,), (1,)), ((), ())), preferred_element_type=jnp.float32
        )

    rot_own = rotate(held, grad)
    rot_other = rotate(held, other_grad)
    rot_own, rot_other = lax.optimization_barrier((rot_own, rot_other))
    partial = jnp.dot(rot_own.astype(jnp.bfloat16), grad, preferred_element_type=jnp.float32)
    partial += jnp.dot(rot_other.astype(jnp.bfloat16), other_grad, preferred_element_type=jnp.float32)
    held_later, partial = lax.optimization_barrier((held, partial))
    whole = jnp.concatenate([held, across(held_later)], 0)
    rot_grad = jnp.concatenate([rot_own, rotate(whole[rot_own.shape[0] :], grad)], 0)
    rot_moment = lax.dot_general(
        whole, moment_next, (((1,), (1,)), ((), ())), preferred_element_type=jnp.float32
    )

    cube = (2,) * bits + (own, rows)
    odd = np.array([half_of(o) for o in range(n // 2)]).reshape((2,) * chip_bits + (1, 1, 1)) == 1

    def flips(value):
        for bit in range(bits):
            axis = bits - 1 - bit
            value = jnp.where((me >> bit) & 1, jnp.flip(value, axis), value)
        return value

    def swap(value):
        return jnp.where(odd, jnp.flip(value, chip_bits), value)

    turns = tuple(tuple(chip_bits - 1 - b for b in reversed(order)) for order in orders)
    rest = (chip_bits, chip_bits + 1)

    def turned(value, turn, back):
        turn = tuple(np.argsort(turn)) if back else turn
        return value.transpose(turn + rest)

    def by_half(first, back):
        pair = [turned(first, turn, back) for turn in turns]
        return jnp.where(my_half == 0, pair[0], pair[1]), jnp.where(my_half == 0, pair[1], pair[0])

    placed = swap(flips(second.T.reshape(cube)))
    mine = by_half(placed[(slice(None),) * chip_bits + (0,)], False)[0]
    theirs = by_half(placed[(slice(None),) * chip_bits + (1,)], False)[1]
    both = jnp.concatenate([mine.reshape(-1, rows), theirs.reshape(-1, rows)], 0)
    both = 0.95 * both + 0.05 * rot_grad * rot_grad
    scaled = (rot_moment / (jnp.sqrt(both) + 1e-08)).astype(jnp.bfloat16)
    both, scaled = lax.optimization_barrier((both, scaled))
    def shrink(partial, step, *beside):
        half = partial.shape[0] // 2
        come = exchange(partial[half:].astype(jnp.bfloat16), step)
        if beside:
            come, *beside = lax.optimization_barrier((come, *beside))
        return partial[:half] + come.astype(jnp.float32), beside

    partial, (both, scaled) = shrink(partial, chip_bits - 1, both, scaled)
    update = lax.dot_general(
        scaled, whole, (((0,), (0,)), ((), ())), preferred_element_type=jnp.float32
    ).astype(jnp.bfloat16)
    partial, (update,) = shrink(partial, chip_bits - 2, update)
    for step in reversed(range(chip_bits - 2)):
        partial, _ = shrink(partial, step)
    basis_next = partial / jnp.sqrt(jnp.mean(partial * partial, axis=1, keepdims=True) + 1e-06)
    count = rot_own.shape[0]
    half_cube = (2,) * chip_bits + (own, rows)
    mine = by_half(both[:count].reshape(half_cube), True)[0]
    theirs = by_half(both[count:].reshape(half_cube), True)[1]
    back = flips(swap(jnp.stack([mine, theirs], chip_bits)))
    second_next = back.reshape(n * own, rows).T
    return update, moment_next, second_next, basis_next


def solution(mesh):
    n = mesh.shape["rows"]
    placed = P(("groups", "rows"), None)
    return jax.shard_map(
        lambda *arrays: shards(n, *arrays),
        mesh=mesh,
        in_specs=(placed,) * 4,
        out_specs=(placed,) * 4,
        check_vma=False,
    )
```

```python
import functools

import jax
import jax.numpy as jnp
from jax import lax
from jax.experimental import pallas as pl
from jax.experimental.pallas import tpu as pltpu
from jax.sharding import PartitionSpec as P

INSIDE = pl.BlockSpec(memory_space=pltpu.VMEM)
ANYWHERE = pl.BlockSpec(memory_space=pl.ANY)
PARAMS = pltpu.CompilerParams(vmem_limit_bytes=24 << 20)


def inside(value):
    return pltpu.with_memory_space_constraint(value, pltpu.VMEM)


def tie(*values):
    return lax.optimization_barrier(values)


def cuts(depth, size):
    return [(at, min(size, depth - at)) for at in range(0, depth, size)]


def odd(i):
    return i.bit_count() & 1


def dot(left, right, dims):
    return lax.dot_general(left, right, (dims, ((), ())), preferred_element_type=jnp.float32)


def moment_kernel(grad, moment, held, stored, sems):
    copies = []
    for i, (at, size) in enumerate(cuts(grad.shape[0], 960)):
        part = pl.ds(at, size)
        held[part] = (
            0.9 * moment[part].astype(jnp.float32) + 0.1 * grad[part].astype(jnp.float32)
        ).astype(jnp.bfloat16)
        copy = pltpu.make_async_copy(held.at[part], stored.at[part], sems.at[i])
        copy.start()
        copies.append(copy)
    for copy in copies:
        copy.wait()


def new_moment(grad, moment):
    return pl.pallas_call(
        moment_kernel,
        in_specs=[INSIDE, INSIDE],
        out_specs=[INSIDE, ANYWHERE],
        out_shape=[
            pltpu.VMEM(grad.shape, grad.dtype),
            jax.ShapeDtypeStruct(grad.shape, grad.dtype),
        ],
        scratch_shapes=[pltpu.SemaphoreType.DMA((len(cuts(grad.shape[0], 960)),))],
        compiler_params=PARAMS,
        name="moment",
    )(inside(grad), inside(moment))


def power_kernel(basis, grad, other, rot, kept, sent):
    rot_own = dot(basis[...], grad[...], ((1,), (0,)))
    rot_other = dot(basis[...], other[...], ((1,), (0,)))
    rot[...] = rot_own
    rot_own = rot_own.astype(jnp.bfloat16)
    rot_other = rot_other.astype(jnp.bfloat16)
    half = kept.shape[0]
    for at, size in cuts(grad.shape[0], 768):
        part = pl.ds(at, size)
        product = dot(rot_own, grad[part], ((1,), (1,))) + dot(rot_other, other[part], ((1,), (1,)))
        kept[:, part] = product[:half]
        sent[:, part] = product[half:].astype(jnp.bfloat16)


def power_products(basis, grad, other):
    count, depth = basis.shape
    rows = grad.shape[1]
    return pl.pallas_call(
        power_kernel,
        in_specs=[INSIDE] * 3,
        out_specs=[INSIDE] * 3,
        out_shape=[
            pltpu.VMEM((count, rows), jnp.float32),
            pltpu.VMEM((count // 2, depth), jnp.float32),
            pltpu.VMEM((count // 2, depth), jnp.bfloat16),
        ],
        compiler_params=PARAMS,
        name="power",
    )(inside(basis), inside(grad), inside(other))


def scale_kernel(orders, own, basis, grad, moment, rot_half, second, scaled, second_next, rot, mom):
    me = lax.axis_index("rows")
    core, chip = me & 1, me >> 1
    bits = len(orders[0])
    parity = functools.reduce(lambda a, b: a ^ b, [(me >> b) & 1 for b in range(bits + 1)])
    count = rot_half.shape[0]
    rot[:count] = rot_half[...]
    rot[count:] = dot(basis[count:], grad[...], ((1,), (0,)))
    mom[...] = dot(basis[...], moment[...], ((1,), (0,)))

    def place(offset, order):
        return sum(((offset >> bit) & 1) << step for step, bit in enumerate(order)) * own

    for half in range(2):

        @pl.when(parity == half)
        def _():
            for offset in range(1 << bits):
                mine = pl.ds(place(offset, orders[half]), own)
                theirs = pl.ds(count + place(offset, orders[1 - half]), own)
                first = core == odd(offset)
                tile = pl.ds(pl.multiple_of((chip ^ offset) * 2 * own, 2 * own), 2 * own)

                def joined(ref):
                    a, b = ref[mine], ref[theirs]
                    return jnp.where(
                        first, jnp.concatenate([a, b], 0), jnp.concatenate([b, a], 0)
                    )

                turned = joined(rot)
                value = 0.95 * second[tile] + 0.05 * turned * turned
                second_next[tile] = value
                ratio = joined(mom) / (jnp.sqrt(value) + 1e-08)
                rot[mine] = jnp.where(first, ratio[:own], ratio[own:])
                rot[theirs] = jnp.where(first, ratio[own:], ratio[:own])

    scaled[...] = rot[...].astype(jnp.bfloat16)


def scaled_rotation(orders, own, basis, grad, moment, rot_half, second):
    count, rows = basis.shape[0], grad.shape[1]
    return pl.pallas_call(
        functools.partial(scale_kernel, orders, own),
        in_specs=[INSIDE] * 5,
        out_specs=[INSIDE] * 2,
        out_shape=[
            pltpu.VMEM((count, rows), jnp.bfloat16),
            jax.ShapeDtypeStruct((count, rows), jnp.float32),
        ],
        scratch_shapes=[pltpu.VMEM((count, rows), jnp.float32)] * 2,
        compiler_params=PARAMS,
        name="scale",
    )(*map(inside, (basis, grad, moment, rot_half, second)))


def update_kernel(basis, scaled, out, held, sems):
    copies = []
    for i, (at, size) in enumerate(cuts(out.shape[0], 640)):
        part = pl.ds(at, size)
        held[part] = dot(basis[:, part], scaled[...], ((0,), (0,))).astype(jnp.bfloat16)
        copy = pltpu.make_async_copy(held.at[part], out.at[part], sems.at[i])
        copy.start()
        copies.append(copy)
    for copy in copies:
        copy.wait()


def new_update(basis, scaled):
    depth, rows = basis.shape[1], scaled.shape[1]
    return pl.pallas_call(
        update_kernel,
        in_specs=[INSIDE] * 2,
        out_specs=ANYWHERE,
        out_shape=jax.ShapeDtypeStruct((depth, rows), jnp.bfloat16),
        scratch_shapes=[
            pltpu.VMEM((depth, rows), jnp.bfloat16),
            pltpu.SemaphoreType.DMA((len(cuts(depth, 640)),)),
        ],
        compiler_params=PARAMS,
        name="update",
    )(inside(basis), inside(scaled))


def shards(n, grad, moment, second, basis):
    bits = n.bit_length() - 2
    own = basis.shape[0]
    orders = (tuple(reversed(range(bits))), (0,) + tuple(reversed(range(1, bits))))

    def exchange(value, step):
        pairs = [(i, i ^ (2 << orders[odd(i)][step]) ^ 1) for i in range(n)]
        return lax.ppermute(value, "rows", pairs)

    def across(value):
        return lax.ppermute(value, "rows", [(i, i ^ 1) for i in range(n)])

    grad, moment, second = grad.T, moment.T, second.T
    other = across(grad.T).T

    held = basis
    for step in range(bits):
        if step == 1:
            held, moment = tie(held, moment)
        come = exchange(held, step)
        if step == 0:
            come, other = tie(come, other)
        if step == 1:
            moment_in, moment_next = new_moment(grad, moment)
            come, moment_in, moment_next = tie(come, moment_in, moment_next)
        held = jnp.concatenate([held, come], 0)

    rot_half, kept, sent = power_products(held, grad, other)
    come = exchange(sent, bits - 1)
    held, _ = tie(held, sent)
    whole = jnp.concatenate([held, across(held)], 0)
    come, whole = tie(come, whole)
    for step in reversed(range(bits)):
        kept = kept + come.astype(jnp.float32)
        if step == 0:
            break
        half = kept.shape[0] // 2
        come = exchange(kept[half:].astype(jnp.bfloat16), step - 1)
        kept = kept[:half]
        if step == bits - 1:
            whole, kept = tie(whole, kept)
            scaled, second_next = scaled_rotation(
                orders, own, whole, grad, moment_in, rot_half, second
            )
            come, scaled, second_next = tie(come, scaled, second_next)
        if step == bits - 2:
            scaled, kept = tie(scaled, kept)
            update = new_update(whole, scaled)
            come, update = tie(come, update)
    basis_next = kept / jnp.sqrt(jnp.mean(kept * kept, axis=1, keepdims=True) + 1e-06)
    return update.T, moment_next.T, second_next.T, basis_next


def solution(mesh):
    n = mesh.shape["rows"]
    placed = P(("groups", "rows"), None)
    return jax.shard_map(
        lambda *arrays: shards(n, *arrays),
        mesh=mesh,
        in_specs=(placed,) * 4,
        out_specs=(placed,) * 4,
        check_vma=False,
    )
```

```python
import functools

import jax
import jax.numpy as jnp
from jax import lax
from jax.experimental import pallas as pl
from jax.experimental.pallas import tpu as pltpu
from jax.sharding import PartitionSpec as P

INSIDE = pl.BlockSpec(memory_space=pltpu.VMEM)
ANYWHERE = pl.BlockSpec(memory_space=pl.ANY)
PARAMS = pltpu.CompilerParams(vmem_limit_bytes=24 << 20)


def inside(value):
    return pltpu.with_memory_space_constraint(value, pltpu.VMEM)


def tie(*values):
    return lax.optimization_barrier(values)


def cuts(depth, size):
    return [(at, min(size, depth - at)) for at in range(0, depth, size)]


def odd(i):
    return i.bit_count() & 1


def dot(left, right, dims):
    return lax.dot_general(left, right, (dims, ((), ())), preferred_element_type=jnp.float32)


def load_kernel(*refs):
    count = len(refs) // 2
    sems = refs[-1]
    copies = [
        pltpu.make_async_copy(refs[i], refs[count + i], sems.at[i]) for i in range(count)
    ]
    for copy in copies:
        copy.start()
    for copy in copies:
        copy.wait()


def load(*values):
    out = pl.pallas_call(
        load_kernel,
        in_specs=[pl.BlockSpec(memory_space=pltpu.HBM)] * len(values),
        out_specs=[INSIDE] * len(values),
        out_shape=[pltpu.VMEM(value.shape, value.dtype) for value in values],
        scratch_shapes=[pltpu.SemaphoreType.DMA((len(values),))],
        compiler_params=PARAMS,
        name="load",
    )(*[pltpu.with_memory_space_constraint(value, pltpu.HBM) for value in values])
    return out


def moment_kernel(grad, moment, held, stored, sems):
    copies = []
    for i, (at, size) in enumerate(cuts(grad.shape[0], 960)):
        part = pl.ds(at, size)
        held[part] = (
            0.9 * moment[part].astype(jnp.float32) + 0.1 * grad[part].astype(jnp.float32)
        ).astype(jnp.bfloat16)
        copy = pltpu.make_async_copy(held.at[part], stored.at[part], sems.at[i])
        copy.start()
        copies.append(copy)
    for copy in copies:
        copy.wait()


def new_moment(grad, moment):
    return pl.pallas_call(
        moment_kernel,
        in_specs=[INSIDE, INSIDE],
        out_specs=[INSIDE, ANYWHERE],
        out_shape=[
            pltpu.VMEM(grad.shape, grad.dtype),
            jax.ShapeDtypeStruct(grad.shape, grad.dtype),
        ],
        scratch_shapes=[pltpu.SemaphoreType.DMA((len(cuts(grad.shape[0], 960)),))],
        compiler_params=PARAMS,
        name="moment",
    )(inside(grad), inside(moment))


def power_kernel(basis, grad, other, rot, kept, sent):
    rot_own = dot(basis[...], grad[...], ((1,), (0,)))
    rot_other = dot(basis[...], other[...], ((1,), (0,)))
    rot[...] = rot_own
    rot_own = rot_own.astype(jnp.bfloat16)
    rot_other = rot_other.astype(jnp.bfloat16)
    half = kept.shape[0]
    for at, size in cuts(grad.shape[0], 768):
        part = pl.ds(at, size)
        product = dot(rot_own, grad[part], ((1,), (1,))) + dot(rot_other, other[part], ((1,), (1,)))
        kept[:, part] = product[:half]
        sent[:, part] = product[half:].astype(jnp.bfloat16)


def power_products(basis, grad, other):
    count, depth = basis.shape
    rows = grad.shape[1]
    return pl.pallas_call(
        power_kernel,
        in_specs=[INSIDE] * 3,
        out_specs=[INSIDE] * 3,
        out_shape=[
            pltpu.VMEM((count, rows), jnp.float32),
            pltpu.VMEM((count // 2, depth), jnp.float32),
            pltpu.VMEM((count // 2, depth), jnp.bfloat16),
        ],
        compiler_params=PARAMS,
        name="power",
    )(inside(basis), inside(grad), inside(other))


def scale_kernel(orders, own, basis, grad, moment, rot_half, second, scaled, second_next, rot, mom):
    me = lax.axis_index("rows")
    core, chip = me & 1, me >> 1
    bits = len(orders[0])
    parity = functools.reduce(lambda a, b: a ^ b, [(me >> b) & 1 for b in range(bits + 1)])
    count = rot_half.shape[0]
    rot[:count] = rot_half[...]
    rot[count:] = dot(basis[count:], grad[...], ((1,), (0,)))
    mom[...] = dot(basis[...], moment[...], ((1,), (0,)))

    def place(offset, order):
        return sum(((offset >> bit) & 1) << step for step, bit in enumerate(order)) * own

    for half in range(2):

        @pl.when(parity == half)
        def _():
            for offset in range(1 << bits):
                mine = pl.ds(place(offset, orders[half]), own)
                theirs = pl.ds(count + place(offset, orders[1 - half]), own)
                first = core == odd(offset)
                tile = pl.ds(pl.multiple_of((chip ^ offset) * 2 * own, 2 * own), 2 * own)

                def joined(ref):
                    a, b = ref[mine], ref[theirs]
                    return jnp.where(
                        first, jnp.concatenate([a, b], 0), jnp.concatenate([b, a], 0)
                    )

                turned = joined(rot)
                value = 0.95 * second[tile] + 0.05 * turned * turned
                second_next[tile] = value
                ratio = joined(mom) / (jnp.sqrt(value) + 1e-08)
                rot[mine] = jnp.where(first, ratio[:own], ratio[own:])
                rot[theirs] = jnp.where(first, ratio[own:], ratio[:own])

    scaled[...] = rot[...].astype(jnp.bfloat16)


def scaled_rotation(orders, own, basis, grad, moment, rot_half, second):
    count, rows = basis.shape[0], grad.shape[1]
    return pl.pallas_call(
        functools.partial(scale_kernel, orders, own),
        in_specs=[INSIDE] * 5,
        out_specs=[INSIDE] * 2,
        out_shape=[
            pltpu.VMEM((count, rows), jnp.bfloat16),
            jax.ShapeDtypeStruct((count, rows), jnp.float32),
        ],
        scratch_shapes=[pltpu.VMEM((count, rows), jnp.float32)] * 2,
        compiler_params=PARAMS,
        name="scale",
    )(*map(inside, (basis, grad, moment, rot_half, second)))


def update_kernel(basis, scaled, out, held, sems):
    copies = []
    for i, (at, size) in enumerate(cuts(out.shape[0], 640)):
        part = pl.ds(at, size)
        held[part] = dot(basis[:, part], scaled[...], ((0,), (0,))).astype(jnp.bfloat16)
        copy = pltpu.make_async_copy(held.at[part], out.at[part], sems.at[i])
        copy.start()
        copies.append(copy)
    for copy in copies:
        copy.wait()


def new_update(basis, scaled):
    depth, rows = basis.shape[1], scaled.shape[1]
    return pl.pallas_call(
        update_kernel,
        in_specs=[INSIDE] * 2,
        out_specs=ANYWHERE,
        out_shape=jax.ShapeDtypeStruct((depth, rows), jnp.bfloat16),
        scratch_shapes=[
            pltpu.VMEM((depth, rows), jnp.bfloat16),
            pltpu.SemaphoreType.DMA((len(cuts(depth, 640)),)),
        ],
        compiler_params=PARAMS,
        name="update",
    )(inside(basis), inside(scaled))


def shards(n, grad, moment, second, basis):
    bits = n.bit_length() - 2
    own = basis.shape[0]
    orders = (tuple(reversed(range(bits))), (0,) + tuple(reversed(range(1, bits))))

    def exchange(value, step):
        pairs = [(i, i ^ (2 << orders[odd(i)][step]) ^ 1) for i in range(n)]
        return lax.ppermute(value, "rows", pairs)

    def across(value):
        return lax.ppermute(value, "rows", [(i, i ^ 1) for i in range(n)])

    grad, moment, second = grad.T, moment.T, second.T

    come = exchange(basis, 0)
    grad, held = load(grad, basis)
    come, grad, held = tie(come, grad, held)
    other = across(grad)
    held = jnp.concatenate([held, come], 0)
    for step in range(1, bits):
        if step == bits - 1:
            held, moment = tie(held, moment)
        come = exchange(held, step)
        if step == bits - 1:
            (moment,) = load(moment)
            come, moment, other = tie(come, moment, other)
        held = jnp.concatenate([held, come], 0)

    rot_half, kept, sent = power_products(held, grad, other)
    come = exchange(sent, bits - 1)
    moment, _ = tie(moment, sent)
    moment_in, moment_next = new_moment(grad, moment)
    held, _ = tie(held, moment_in)
    theirs = across(held)
    come, moment_in, moment_next = tie(come, moment_in, moment_next)
    for step in reversed(range(bits)):
        kept = kept + come.astype(jnp.float32)
        if step == 0:
            break
        half = kept.shape[0] // 2
        come = exchange(kept[half:].astype(jnp.bfloat16), step - 1)
        kept = kept[:half]
        if step == bits - 1:
            theirs, kept = tie(theirs, kept)
            whole = jnp.concatenate([held, theirs], 0)
            scaled, second_next = scaled_rotation(
                orders, own, whole, grad, moment_in, rot_half, second
            )
            come, scaled, second_next = tie(come, scaled, second_next)
        if step == bits - 2:
            scaled, kept = tie(scaled, kept)
            update = new_update(whole, scaled)
            come, update = tie(come, update)
    basis_next = kept / jnp.sqrt(jnp.mean(kept * kept, axis=1, keepdims=True) + 1e-06)
    return update.T, moment_next.T, second_next.T, basis_next


def solution(mesh):
    n = mesh.shape["rows"]
    placed = P(("groups", "rows"), None)
    return jax.shard_map(
        lambda *arrays: shards(n, *arrays),
        mesh=mesh,
        in_specs=(placed,) * 4,
        out_specs=(placed,) * 4,
        check_vma=False,
    )
```

```python
import functools

import jax
import jax.numpy as jnp
from jax import lax
from jax.experimental import pallas as pl
from jax.experimental.pallas import tpu as pltpu
from jax.sharding import PartitionSpec as P

INSIDE = pl.BlockSpec(memory_space=pltpu.VMEM)
ANYWHERE = pl.BlockSpec(memory_space=pl.ANY)
PARAMS = pltpu.CompilerParams(vmem_limit_bytes=24 << 20)


def inside(value):
    return pltpu.with_memory_space_constraint(value, pltpu.VMEM)


def tie(*values):
    return lax.optimization_barrier(values)


def cuts(depth, size):
    return [(at, min(size, depth - at)) for at in range(0, depth, size)]


def odd(i):
    return i.bit_count() & 1


def dot(left, right, dims):
    return lax.dot_general(left, right, (dims, ((), ())), preferred_element_type=jnp.float32)


def load_kernel(*refs):
    count = len(refs) // 2
    sems = refs[-1]
    copies = [
        pltpu.make_async_copy(refs[i], refs[count + i], sems.at[i]) for i in range(count)
    ]
    for copy in copies:
        copy.start()
    for copy in copies:
        copy.wait()


def load(*values):
    out = pl.pallas_call(
        load_kernel,
        in_specs=[pl.BlockSpec(memory_space=pltpu.HBM)] * len(values),
        out_specs=[INSIDE] * len(values),
        out_shape=[pltpu.VMEM(value.shape, value.dtype) for value in values],
        scratch_shapes=[pltpu.SemaphoreType.DMA((len(values),))],
        compiler_params=PARAMS,
        name="load",
    )(*[pltpu.with_memory_space_constraint(value, pltpu.HBM) for value in values])
    return out


def moment_kernel(grad, moment, held, stored, sems):
    copies = []
    for i, (at, size) in enumerate(cuts(grad.shape[0], 960)):
        part = pl.ds(at, size)
        held[part] = (
            0.9 * moment[part].astype(jnp.float32) + 0.1 * grad[part].astype(jnp.float32)
        ).astype(jnp.bfloat16)
        copy = pltpu.make_async_copy(held.at[part], stored.at[part], sems.at[i])
        copy.start()
        copies.append(copy)
    for copy in copies:
        copy.wait()


def new_moment(grad, moment):
    return pl.pallas_call(
        moment_kernel,
        in_specs=[INSIDE, INSIDE],
        out_specs=[INSIDE, ANYWHERE],
        out_shape=[
            pltpu.VMEM(grad.shape, grad.dtype),
            jax.ShapeDtypeStruct(grad.shape, grad.dtype),
        ],
        scratch_shapes=[pltpu.SemaphoreType.DMA((len(cuts(grad.shape[0], 960)),))],
        compiler_params=PARAMS,
        name="moment",
    )(inside(grad), inside(moment))


def power_kernel(basis, grad, other, rot, kept, sent):
    rot_own = dot(basis[...], grad[...], ((1,), (0,)))
    rot_other = dot(basis[...], other[...], ((1,), (0,)))
    rot[...] = rot_own
    rot_own = rot_own.astype(jnp.bfloat16)
    rot_other = rot_other.astype(jnp.bfloat16)
    half = kept.shape[0]
    for at, size in cuts(grad.shape[0], 768):
        part = pl.ds(at, size)
        product = dot(rot_own, grad[part], ((1,), (1,))) + dot(rot_other, other[part], ((1,), (1,)))
        kept[:, part] = product[:half]
        sent[:, part] = product[half:].astype(jnp.bfloat16)


def power_products(basis, grad, other):
    count, depth = basis.shape
    rows = grad.shape[1]
    return pl.pallas_call(
        power_kernel,
        in_specs=[INSIDE] * 3,
        out_specs=[INSIDE] * 3,
        out_shape=[
            pltpu.VMEM((count, rows), jnp.float32),
            pltpu.VMEM((count // 2, depth), jnp.float32),
            pltpu.VMEM((count // 2, depth), jnp.bfloat16),
        ],
        compiler_params=PARAMS,
        name="power",
    )(inside(basis), inside(grad), inside(other))


def scale_kernel(orders, own, basis, grad, moment, rot_half, second, scaled, second_next, rot, mom):
    me = lax.axis_index("rows")
    core, chip = me & 1, me >> 1
    bits = len(orders[0])
    parity = functools.reduce(lambda a, b: a ^ b, [(me >> b) & 1 for b in range(bits + 1)])
    count = rot_half.shape[0]
    rot[:count] = rot_half[...]
    rot[count:] = dot(basis[count:], grad[...], ((1,), (0,)))
    mom[...] = dot(basis[...], moment[...], ((1,), (0,)))

    def place(offset, order):
        return sum(((offset >> bit) & 1) << step for step, bit in enumerate(order)) * own

    for half in range(2):

        @pl.when(parity == half)
        def _():
            for offset in range(1 << bits):
                mine = pl.ds(place(offset, orders[half]), own)
                theirs = pl.ds(count + place(offset, orders[1 - half]), own)
                first = core == odd(offset)
                tile = pl.ds(pl.multiple_of((chip ^ offset) * 2 * own, 2 * own), 2 * own)

                def joined(ref):
                    a, b = ref[mine], ref[theirs]
                    return jnp.where(
                        first, jnp.concatenate([a, b], 0), jnp.concatenate([b, a], 0)
                    )

                turned = joined(rot)
                value = 0.95 * second[tile] + 0.05 * turned * turned
                second_next[tile] = value
                ratio = joined(mom) / (jnp.sqrt(value) + 1e-08)
                rot[mine] = jnp.where(first, ratio[:own], ratio[own:])
                rot[theirs] = jnp.where(first, ratio[own:], ratio[:own])

    scaled[...] = rot[...].astype(jnp.bfloat16)


def scaled_rotation(orders, own, basis, grad, moment, rot_half, second):
    count, rows = basis.shape[0], grad.shape[1]
    return pl.pallas_call(
        functools.partial(scale_kernel, orders, own),
        in_specs=[INSIDE] * 5,
        out_specs=[INSIDE] * 2,
        out_shape=[
            pltpu.VMEM((count, rows), jnp.bfloat16),
            jax.ShapeDtypeStruct((count, rows), jnp.float32),
        ],
        scratch_shapes=[pltpu.VMEM((count, rows), jnp.float32)] * 2,
        compiler_params=PARAMS,
        name="scale",
    )(*map(inside, (basis, grad, moment, rot_half, second)))


def update_kernel(basis, scaled, out, held, sems):
    copies = []
    for i, (at, size) in enumerate(cuts(out.shape[0], 640)):
        part = pl.ds(at, size)
        held[part] = dot(basis[:, part], scaled[...], ((0,), (0,))).astype(jnp.bfloat16)
        copy = pltpu.make_async_copy(held.at[part], out.at[part], sems.at[i])
        copy.start()
        copies.append(copy)
    for copy in copies:
        copy.wait()


def new_update(basis, scaled):
    depth, rows = basis.shape[1], scaled.shape[1]
    return pl.pallas_call(
        update_kernel,
        in_specs=[INSIDE] * 2,
        out_specs=ANYWHERE,
        out_shape=jax.ShapeDtypeStruct((depth, rows), jnp.bfloat16),
        scratch_shapes=[
            pltpu.VMEM((depth, rows), jnp.bfloat16),
            pltpu.SemaphoreType.DMA((len(cuts(depth, 640)),)),
        ],
        compiler_params=PARAMS,
        name="update",
    )(inside(basis), inside(scaled))


def shards(n, grad, moment, second, basis):
    bits = n.bit_length() - 2
    own = basis.shape[0]
    far, near = (bits - 1,), tuple(reversed(range(bits - 1)))
    orders = (far + near, far + near[-1:] + near[:-1])

    def exchange(value, step):
        pairs = [(i, i ^ (2 << orders[odd(i)][step]) ^ 1) for i in range(n)]
        return lax.ppermute(value, "rows", pairs)

    def across(value):
        return lax.ppermute(value, "rows", [(i, i ^ 1) for i in range(n)])

    grad, moment, second = grad.T, moment.T, second.T

    come = exchange(basis, 0)
    grad, held = load(grad, basis)
    come, grad, held = tie(come, grad, held)
    other = across(grad)
    held = jnp.concatenate([held, come], 0)
    for step in range(1, bits):
        if step == bits - 1:
            held, moment = tie(held, moment)
        come = exchange(held, step)
        if step == bits - 1:
            (moment,) = load(moment)
            come, moment, other = tie(come, moment, other)
        held = jnp.concatenate([held, come], 0)

    rot_half, kept, sent = power_products(held, grad, other)
    come = exchange(sent, bits - 1)
    moment, _ = tie(moment, sent)
    moment_in, moment_next = new_moment(grad, moment)
    held, _ = tie(held, moment_in)
    theirs = across(held)
    come, moment_in, moment_next = tie(come, moment_in, moment_next)
    for step in reversed(range(bits)):
        kept = kept + come.astype(jnp.float32)
        if step == 0:
            break
        half = kept.shape[0] // 2
        come = exchange(kept[half:].astype(jnp.bfloat16), step - 1)
        kept = kept[:half]
        if step == bits - 1:
            theirs, kept = tie(theirs, kept)
            whole = jnp.concatenate([held, theirs], 0)
            scaled, second_next = scaled_rotation(
                orders, own, whole, grad, moment_in, rot_half, second
            )
            come, scaled, second_next = tie(come, scaled, second_next)
        if step == bits - 2:
            scaled, kept = tie(scaled, kept)
            update = new_update(whole, scaled)
            come, update = tie(come, update)
    basis_next = kept / jnp.sqrt(jnp.mean(kept * kept, axis=1, keepdims=True) + 1e-06)
    return update.T, moment_next.T, second_next.T, basis_next


def solution(mesh):
    n = mesh.shape["rows"]
    placed = P(("groups", "rows"), None)
    return jax.shard_map(
        lambda *arrays: shards(n, *arrays),
        mesh=mesh,
        in_specs=(placed,) * 4,
        out_specs=(placed,) * 4,
        check_vma=False,
    )
```

```python
import functools

import jax
import jax.numpy as jnp
from jax import lax
from jax.experimental import pallas as pl
from jax.experimental.pallas import tpu as pltpu
from jax.sharding import PartitionSpec as P

INSIDE = pl.BlockSpec(memory_space=pltpu.VMEM)
ANYWHERE = pl.BlockSpec(memory_space=pl.ANY)
PARAMS = pltpu.CompilerParams(vmem_limit_bytes=24 << 20)


def inside(value):
    return pltpu.with_memory_space_constraint(value, pltpu.VMEM)


def tie(*values):
    return lax.optimization_barrier(values)


def cuts(depth, size):
    return [(at, min(size, depth - at)) for at in range(0, depth, size)]


def odd(i):
    return i.bit_count() & 1


def dot(left, right, dims):
    return lax.dot_general(left, right, (dims, ((), ())), preferred_element_type=jnp.float32)


def load_kernel(*refs):
    count = len(refs) // 2
    sems = refs[-1]
    copies = [
        pltpu.make_async_copy(refs[i], refs[count + i], sems.at[i]) for i in range(count)
    ]
    for copy in copies:
        copy.start()
    for copy in copies:
        copy.wait()


def load(*values):
    out = pl.pallas_call(
        load_kernel,
        in_specs=[pl.BlockSpec(memory_space=pltpu.HBM)] * len(values),
        out_specs=[INSIDE] * len(values),
        out_shape=[pltpu.VMEM(value.shape, value.dtype) for value in values],
        scratch_shapes=[pltpu.SemaphoreType.DMA((len(values),))],
        compiler_params=PARAMS,
        name="load",
    )(*[pltpu.with_memory_space_constraint(value, pltpu.HBM) for value in values])
    return out


def moment_kernel(grad, moment, held, stored, sems):
    copies = []
    for i, (at, size) in enumerate(cuts(grad.shape[0], 960)):
        part = pl.ds(at, size)
        held[part] = (
            0.9 * moment[part].astype(jnp.float32) + 0.1 * grad[part].astype(jnp.float32)
        ).astype(jnp.bfloat16)
        copy = pltpu.make_async_copy(held.at[part], stored.at[part], sems.at[i])
        copy.start()
        copies.append(copy)
    for copy in copies:
        copy.wait()


def new_moment(grad, moment):
    return pl.pallas_call(
        moment_kernel,
        in_specs=[INSIDE, INSIDE],
        out_specs=[INSIDE, ANYWHERE],
        out_shape=[
            pltpu.VMEM(grad.shape, grad.dtype),
            jax.ShapeDtypeStruct(grad.shape, grad.dtype),
        ],
        scratch_shapes=[pltpu.SemaphoreType.DMA((len(cuts(grad.shape[0], 960)),))],
        compiler_params=PARAMS,
        name="moment",
    )(inside(grad), inside(moment))


def transpose_kernel(value, out):
    out[...] = value[...].T


def transposed(value):
    return pl.pallas_call(
        transpose_kernel,
        in_specs=[INSIDE],
        out_specs=INSIDE,
        out_shape=pltpu.VMEM(value.shape[::-1], value.dtype),
        compiler_params=PARAMS,
        name="transpose",
    )(inside(value))


def power_kernel(basis, grad, other, grad_rows, other_rows, rot, kept, sent):
    rot_own = dot(basis[...], grad[...], ((1,), (0,)))
    rot_other = dot(basis[...], other[...], ((1,), (0,)))
    rot[...] = rot_own
    both = jnp.concatenate([rot_own, rot_other], 1).astype(jnp.bfloat16)
    half = kept.shape[0]
    for at, size in cuts(grad.shape[0], 768):
        part = pl.ds(at, size)
        rows = jnp.concatenate([grad_rows[:, part], other_rows[:, part]], 0)
        product = dot(both, rows, ((1,), (0,)))
        kept[:, part] = product[:half]
        sent[:, part] = product[half:].astype(jnp.bfloat16)


def power_products(*operands):
    basis, grad = operands[:2]
    count, depth = basis.shape
    rows = grad.shape[1]
    return pl.pallas_call(
        power_kernel,
        in_specs=[INSIDE] * len(operands),
        out_specs=[INSIDE] * 3,
        out_shape=[
            pltpu.VMEM((count, rows), jnp.float32),
            pltpu.VMEM((count // 2, depth), jnp.float32),
            pltpu.VMEM((count // 2, depth), jnp.bfloat16),
        ],
        compiler_params=PARAMS,
        name="power",
    )(*map(inside, operands))


def scale_kernel(orders, own, basis, grad, moment, rot_half, second, scaled, second_next, rot, mom):
    me = lax.axis_index("rows")
    core, chip = me & 1, me >> 1
    bits = len(orders[0])
    parity = functools.reduce(lambda a, b: a ^ b, [(me >> b) & 1 for b in range(bits + 1)])
    count = rot_half.shape[0]
    rot[:count] = rot_half[...]
    rot[count:] = dot(basis[count:], grad[...], ((1,), (0,)))
    mom[...] = dot(basis[...], moment[...], ((1,), (0,)))

    def place(offset, order):
        return sum(((offset >> bit) & 1) << step for step, bit in enumerate(order)) * own

    for half in range(2):

        @pl.when(parity == half)
        def _():
            for offset in range(1 << bits):
                mine = pl.ds(place(offset, orders[half]), own)
                theirs = pl.ds(count + place(offset, orders[1 - half]), own)
                first = core == odd(offset)
                tile = pl.ds(pl.multiple_of((chip ^ offset) * 2 * own, 2 * own), 2 * own)

                def joined(ref):
                    a, b = ref[mine], ref[theirs]
                    return jnp.where(
                        first, jnp.concatenate([a, b], 0), jnp.concatenate([b, a], 0)
                    )

                turned = joined(rot)
                value = 0.95 * second[tile] + 0.05 * turned * turned
                second_next[tile] = value
                ratio = joined(mom) / (jnp.sqrt(value) + 1e-08)
                rot[mine] = jnp.where(first, ratio[:own], ratio[own:])
                rot[theirs] = jnp.where(first, ratio[own:], ratio[:own])

    scaled[...] = rot[...].astype(jnp.bfloat16)


def scaled_rotation(orders, own, basis, grad, moment, rot_half, second):
    count, rows = basis.shape[0], grad.shape[1]
    return pl.pallas_call(
        functools.partial(scale_kernel, orders, own),
        in_specs=[INSIDE] * 5,
        out_specs=[INSIDE] * 2,
        out_shape=[
            pltpu.VMEM((count, rows), jnp.bfloat16),
            jax.ShapeDtypeStruct((count, rows), jnp.float32),
        ],
        scratch_shapes=[pltpu.VMEM((count, rows), jnp.float32)] * 2,
        compiler_params=PARAMS,
        name="scale",
    )(*map(inside, (basis, grad, moment, rot_half, second)))


def update_kernel(basis, scaled, out, held, sems):
    copies = []
    for i, (at, size) in enumerate(cuts(out.shape[0], 640)):
        part = pl.ds(at, size)
        held[part] = dot(basis[:, part], scaled[...], ((0,), (0,))).astype(jnp.bfloat16)
        copy = pltpu.make_async_copy(held.at[part], out.at[part], sems.at[i])
        copy.start()
        copies.append(copy)
    for copy in copies:
        copy.wait()


def new_update(basis, scaled):
    depth, rows = basis.shape[1], scaled.shape[1]
    return pl.pallas_call(
        update_kernel,
        in_specs=[INSIDE] * 2,
        out_specs=ANYWHERE,
        out_shape=jax.ShapeDtypeStruct((depth, rows), jnp.bfloat16),
        scratch_shapes=[
            pltpu.VMEM((depth, rows), jnp.bfloat16),
            pltpu.SemaphoreType.DMA((len(cuts(depth, 640)),)),
        ],
        compiler_params=PARAMS,
        name="update",
    )(inside(basis), inside(scaled))


def shards(n, grad, moment, second, basis):
    bits = n.bit_length() - 2
    own = basis.shape[0]
    far, near = (bits - 1,), tuple(reversed(range(bits - 1)))
    orders = (far + near, far + near[-1:] + near[:-1])

    def exchange(value, step):
        pairs = [(i, i ^ (2 << orders[odd(i)][step]) ^ 1) for i in range(n)]
        return lax.ppermute(value, "rows", pairs)

    def across(value):
        return lax.ppermute(value, "rows", [(i, i ^ 1) for i in range(n)])

    grad, moment, second = grad.T, moment.T, second.T

    come = exchange(basis, 0)
    grad, held = load(grad, basis)
    come, grad, held = tie(come, grad, held)
    other = across(grad)
    held = jnp.concatenate([held, come], 0)
    for step in range(1, bits):
        if step == 1:
            held, grad = tie(held, grad)
        if step == bits - 1:
            held, moment = tie(held, moment)
        come = exchange(held, step)
        if step == 1:
            grad_rows = transposed(grad)
            come, grad_rows = tie(come, grad_rows)
        if step == bits - 1:
            (moment,) = load(moment)
            moment, other = tie(moment, other)
            other_rows = transposed(other)
            come, moment, other, other_rows = tie(come, moment, other, other_rows)
        held = jnp.concatenate([held, come], 0)

    rot_half, kept, sent = power_products(held, grad, other, grad_rows, other_rows)
    come = exchange(sent, bits - 1)
    moment, _ = tie(moment, sent)
    moment_in, moment_next = new_moment(grad, moment)
    held, _ = tie(held, moment_in)
    theirs = across(held)
    come, moment_in, moment_next = tie(come, moment_in, moment_next)
    for step in reversed(range(bits)):
        kept = kept + come.astype(jnp.float32)
        if step == 0:
            break
        half = kept.shape[0] // 2
        come = exchange(kept[half:].astype(jnp.bfloat16), step - 1)
        kept = kept[:half]
        if step == bits - 1:
            theirs, kept = tie(theirs, kept)
            whole = jnp.concatenate([held, theirs], 0)
            scaled, second_next = scaled_rotation(
                orders, own, whole, grad, moment_in, rot_half, second
            )
            come, scaled, second_next = tie(come, scaled, second_next)
        if step == bits - 2:
            scaled, kept = tie(scaled, kept)
            update = new_update(whole, scaled)
            come, update = tie(come, update)
    basis_next = kept / jnp.sqrt(jnp.mean(kept * kept, axis=1, keepdims=True) + 1e-06)
    return update.T, moment_next.T, second_next.T, basis_next


def solution(mesh):
    n = mesh.shape["rows"]
    placed = P(("groups", "rows"), None)
    return jax.shard_map(
        lambda *arrays: shards(n, *arrays),
        mesh=mesh,
        in_specs=(placed,) * 4,
        out_specs=(placed,) * 4,
        check_vma=False,
    )
```

```python
import functools

import jax
import jax.numpy as jnp
from jax import lax
from jax.experimental import pallas as pl
from jax.experimental.pallas import tpu as pltpu
from jax.sharding import PartitionSpec as P

INSIDE = pl.BlockSpec(memory_space=pltpu.VMEM)
ANYWHERE = pl.BlockSpec(memory_space=pl.ANY)
PARAMS = pltpu.CompilerParams(vmem_limit_bytes=24 << 20)


def inside(value):
    return pltpu.with_memory_space_constraint(value, pltpu.VMEM)


def tie(*values):
    return lax.optimization_barrier(values)


def cuts(depth, size):
    return [(at, min(size, depth - at)) for at in range(0, depth, size)]


def odd(i):
    return i.bit_count() & 1


def dot(left, right, dims):
    return lax.dot_general(left, right, (dims, ((), ())), preferred_element_type=jnp.float32)


def load_kernel(*refs):
    count = len(refs) // 2
    sems = refs[-1]
    copies = [
        pltpu.make_async_copy(refs[i], refs[count + i], sems.at[i]) for i in range(count)
    ]
    for copy in copies:
        copy.start()
    for copy in copies:
        copy.wait()


def load(*values):
    out = pl.pallas_call(
        load_kernel,
        in_specs=[pl.BlockSpec(memory_space=pltpu.HBM)] * len(values),
        out_specs=[INSIDE] * len(values),
        out_shape=[pltpu.VMEM(value.shape, value.dtype) for value in values],
        scratch_shapes=[pltpu.SemaphoreType.DMA((len(values),))],
        compiler_params=PARAMS,
        name="load",
    )(*[pltpu.with_memory_space_constraint(value, pltpu.HBM) for value in values])
    return out


def moment_kernel(grad, moment, held, stored, sems):
    copies = []
    for i, (at, size) in enumerate(cuts(grad.shape[0], 960)):
        part = pl.ds(at, size)
        held[part] = (
            0.9 * moment[part].astype(jnp.float32) + 0.1 * grad[part].astype(jnp.float32)
        ).astype(jnp.bfloat16)
        copy = pltpu.make_async_copy(held.at[part], stored.at[part], sems.at[i])
        copy.start()
        copies.append(copy)
    for copy in copies:
        copy.wait()


def new_moment(grad, moment):
    return pl.pallas_call(
        moment_kernel,
        in_specs=[INSIDE, INSIDE],
        out_specs=[INSIDE, ANYWHERE],
        out_shape=[
            pltpu.VMEM(grad.shape, grad.dtype),
            jax.ShapeDtypeStruct(grad.shape, grad.dtype),
        ],
        scratch_shapes=[pltpu.SemaphoreType.DMA((len(cuts(grad.shape[0], 960)),))],
        compiler_params=PARAMS,
        name="moment",
    )(inside(grad), inside(moment))


def transpose_kernel(*refs):
    count = len(refs) // 2
    for value, out in zip(refs[:count], refs[count:]):
        out[...] = value[...].T


def transposed(*values):
    return pl.pallas_call(
        transpose_kernel,
        in_specs=[INSIDE] * len(values),
        out_specs=[INSIDE] * len(values),
        out_shape=[pltpu.VMEM(value.shape[::-1], value.dtype) for value in values],
        compiler_params=PARAMS,
        name="transpose",
    )(*map(inside, values))


def power_kernel(*refs):
    *pieces, grad, other, grad_rows, other_rows, basis, rot, kept, sent = refs
    basis[...] = jnp.concatenate([piece[...] for piece in pieces], 0)
    rot_own = dot(basis[...], grad[...], ((1,), (0,)))
    rot_other = dot(basis[...], other[...], ((1,), (0,)))
    rot[...] = rot_own
    both = jnp.concatenate([rot_own, rot_other], 1).astype(jnp.bfloat16)
    half = kept.shape[0]
    for at, size in cuts(grad.shape[0], 768):
        part = pl.ds(at, size)
        rows = jnp.concatenate([grad_rows[:, part], other_rows[:, part]], 0)
        product = dot(both, rows, ((1,), (0,)))
        kept[:, part] = product[:half]
        sent[:, part] = product[half:].astype(jnp.bfloat16)


def power_products(pieces, grads):
    depth, rows = grads[0].shape
    count = sum(piece.shape[0] for piece in pieces)
    return pl.pallas_call(
        power_kernel,
        in_specs=[INSIDE] * (len(pieces) + len(grads)),
        out_specs=[INSIDE] * 4,
        out_shape=[
            pltpu.VMEM((count, depth), jnp.bfloat16),
            pltpu.VMEM((count, rows), jnp.float32),
            pltpu.VMEM((count // 2, depth), jnp.float32),
            pltpu.VMEM((count // 2, depth), jnp.bfloat16),
        ],
        compiler_params=PARAMS,
        name="power",
    )(*map(inside, (*pieces, *grads)))


def normal_kernel(kept, come, out):
    power = kept[...] + come[...].astype(jnp.float32)
    square = jnp.mean(power * power, axis=1, keepdims=True)
    out[...] = power / jnp.sqrt(square + 1e-06)


def normalised(kept, come):
    return pl.pallas_call(
        normal_kernel,
        in_specs=[INSIDE] * 2,
        out_specs=INSIDE,
        out_shape=jax.ShapeDtypeStruct(kept.shape, kept.dtype),
        compiler_params=PARAMS,
        name="normalise",
    )(inside(kept), inside(come))


def scale_kernel(orders, own, basis, grad, moment, rot_half, second, scaled, second_next, rot, mom):
    me = lax.axis_index("rows")
    core, chip = me & 1, me >> 1
    bits = len(orders[0])
    parity = functools.reduce(lambda a, b: a ^ b, [(me >> b) & 1 for b in range(bits + 1)])
    count = rot_half.shape[0]
    rot[:count] = rot_half[...]
    rot[count:] = dot(basis[count:], grad[...], ((1,), (0,)))
    mom[...] = dot(basis[...], moment[...], ((1,), (0,)))

    def place(offset, order):
        return sum(((offset >> bit) & 1) << step for step, bit in enumerate(order)) * own

    for half in range(2):

        @pl.when(parity == half)
        def _():
            for offset in range(1 << bits):
                mine = pl.ds(place(offset, orders[half]), own)
                theirs = pl.ds(count + place(offset, orders[1 - half]), own)
                first = core == odd(offset)
                tile = pl.ds(pl.multiple_of((chip ^ offset) * 2 * own, 2 * own), 2 * own)

                def joined(ref):
                    a, b = ref[mine], ref[theirs]
                    return jnp.where(
                        first, jnp.concatenate([a, b], 0), jnp.concatenate([b, a], 0)
                    )

                turned = joined(rot)
                value = 0.95 * second[tile] + 0.05 * turned * turned
                second_next[tile] = value
                ratio = joined(mom) / (jnp.sqrt(value) + 1e-08)
                rot[mine] = jnp.where(first, ratio[:own], ratio[own:])
                rot[theirs] = jnp.where(first, ratio[own:], ratio[:own])

    scaled[...] = rot[...].astype(jnp.bfloat16)


def scaled_rotation(orders, own, basis, grad, moment, rot_half, second):
    count, rows = basis.shape[0], grad.shape[1]
    return pl.pallas_call(
        functools.partial(scale_kernel, orders, own),
        in_specs=[INSIDE] * 5,
        out_specs=[INSIDE] * 2,
        out_shape=[
            pltpu.VMEM((count, rows), jnp.bfloat16),
            jax.ShapeDtypeStruct((count, rows), jnp.float32),
        ],
        scratch_shapes=[pltpu.VMEM((count, rows), jnp.float32)] * 2,
        compiler_params=PARAMS,
        name="scale",
    )(*map(inside, (basis, grad, moment, rot_half, second)))


def update_kernel(basis, scaled, out, held, sems):
    copies = []
    for i, (at, size) in enumerate(cuts(out.shape[0], 640)):
        part = pl.ds(at, size)
        held[part] = dot(basis[:, part], scaled[...], ((0,), (0,))).astype(jnp.bfloat16)
        copy = pltpu.make_async_copy(held.at[part], out.at[part], sems.at[i])
        copy.start()
        copies.append(copy)
    for copy in copies:
        copy.wait()


def new_update(basis, scaled):
    depth, rows = basis.shape[1], scaled.shape[1]
    return pl.pallas_call(
        update_kernel,
        in_specs=[INSIDE] * 2,
        out_specs=ANYWHERE,
        out_shape=jax.ShapeDtypeStruct((depth, rows), jnp.bfloat16),
        scratch_shapes=[
            pltpu.VMEM((depth, rows), jnp.bfloat16),
            pltpu.SemaphoreType.DMA((len(cuts(depth, 640)),)),
        ],
        compiler_params=PARAMS,
        name="update",
    )(inside(basis), inside(scaled))


def shards(n, grad, moment, second, basis):
    bits = n.bit_length() - 2
    own = basis.shape[0]
    far, near = (bits - 1,), tuple(reversed(range(bits - 1)))
    orders = (far + near, far + near[-1:] + near[:-1])

    def exchange(value, step):
        pairs = [(i, i ^ (2 << orders[odd(i)][step]) ^ 1) for i in range(n)]
        return lax.ppermute(value, "rows", pairs)

    def across(value):
        return lax.ppermute(value, "rows", [(i, i ^ 1) for i in range(n)])

    grad, moment, second = grad.T, moment.T, second.T

    come = exchange(basis, 0)
    grad, held = load(grad, basis)
    come, grad, held = tie(come, grad, held)
    other = across(grad)
    held = jnp.concatenate([held, come], 0)
    for step in range(1, bits - 2):
        held = jnp.concatenate([held, exchange(held, step)], 0)
    first = exchange(held, bits - 2)
    second_hand = exchange(held, bits - 1)
    first, grad = tie(first, grad)
    last = exchange(first, bits - 1)
    second_hand, grad, other = tie(second_hand, grad, other)
    grad_rows, other_rows = transposed(grad, other)
    last, grad_rows, other_rows = tie(last, grad_rows, other_rows)
    held, rot_half, kept, sent = power_products(
        (held, first, second_hand, last), (grad, other, grad_rows, other_rows)
    )
    come = exchange(sent, bits - 1)
    moment, _ = tie(moment, sent)
    moment_in, moment_next = new_moment(grad, moment)
    held, _ = tie(held, moment_in)
    theirs = across(held)
    come, moment_in, moment_next = tie(come, moment_in, moment_next)
    for step in reversed(range(bits)):
        if step == 0:
            break
        kept = kept + come.astype(jnp.float32)
        half = kept.shape[0] // 2
        come = exchange(kept[half:].astype(jnp.bfloat16), step - 1)
        kept = kept[:half]
        if step == bits - 1:
            theirs, kept = tie(theirs, kept)
            whole = jnp.concatenate([held, theirs], 0)
            scaled, second_next = scaled_rotation(
                orders, own, whole, grad, moment_in, rot_half, second
            )
            come, scaled, second_next = tie(come, scaled, second_next)
        if step == bits - 2:
            scaled, kept = tie(scaled, kept)
            update = new_update(whole, scaled)
            come, update = tie(come, update)
    basis_next = normalised(kept, come)
    return update.T, moment_next.T, second_next.T, basis_next


def solution(mesh):
    n = mesh.shape["rows"]
    placed = P(("groups", "rows"), None)
    return jax.shard_map(
        lambda *arrays: shards(n, *arrays),
        mesh=mesh,
        in_specs=(placed,) * 4,
        out_specs=(placed,) * 4,
        check_vma=False,
    )
```

```python
import functools

import jax
import jax.numpy as jnp
from jax import lax
from jax.experimental import pallas as pl
from jax.experimental.pallas import tpu as pltpu
from jax.sharding import PartitionSpec as P

INSIDE = pl.BlockSpec(memory_space=pltpu.VMEM)
ANYWHERE = pl.BlockSpec(memory_space=pl.ANY)
PARAMS = pltpu.CompilerParams(vmem_limit_bytes=24 << 20)


def inside(value):
    return pltpu.with_memory_space_constraint(value, pltpu.VMEM)


def tie(*values):
    return lax.optimization_barrier(values)


def cuts(depth, size):
    return [(at, min(size, depth - at)) for at in range(0, depth, size)]


def odd(i):
    return i.bit_count() & 1


def dot(left, right, dims):
    return lax.dot_general(left, right, (dims, ((), ())), preferred_element_type=jnp.float32)


def load_kernel(*refs):
    count = len(refs) // 2
    sems = refs[-1]
    copies = [
        pltpu.make_async_copy(refs[i], refs[count + i], sems.at[i]) for i in range(count)
    ]
    for copy in copies:
        copy.start()
    for copy in copies:
        copy.wait()


def load(*values):
    out = pl.pallas_call(
        load_kernel,
        in_specs=[pl.BlockSpec(memory_space=pltpu.HBM)] * len(values),
        out_specs=[INSIDE] * len(values),
        out_shape=[pltpu.VMEM(value.shape, value.dtype) for value in values],
        scratch_shapes=[pltpu.SemaphoreType.DMA((len(values),))],
        compiler_params=PARAMS,
        name="load",
    )(*[pltpu.with_memory_space_constraint(value, pltpu.HBM) for value in values])
    return out


def moment_kernel(grad, moment, out):
    out[...] = (0.9 * moment[...].astype(jnp.float32) + 0.1 * grad[...].astype(jnp.float32)).astype(
        jnp.bfloat16
    )


def new_moment(grad, moment):
    return pl.pallas_call(
        moment_kernel,
        in_specs=[INSIDE, INSIDE],
        out_specs=INSIDE,
        out_shape=pltpu.VMEM(grad.shape, grad.dtype),
        compiler_params=PARAMS,
        name="moment",
    )(inside(grad), inside(moment))


def transpose_kernel(*refs):
    count = len(refs) // 2
    for value, out in zip(refs[:count], refs[count:]):
        out[...] = value[...].T


def transposed(*values):
    return pl.pallas_call(
        transpose_kernel,
        in_specs=[INSIDE] * len(values),
        out_specs=[INSIDE] * len(values),
        out_shape=[pltpu.VMEM(value.shape[::-1], value.dtype) for value in values],
        compiler_params=PARAMS,
        name="transpose",
    )(*map(inside, values))


def power_kernel(*refs):
    *pieces, grad, other, grad_rows, other_rows, basis, rot, kept, sent, passed = refs
    basis[...] = jnp.concatenate([piece[...] for piece in pieces], 0)
    rot_own = dot(basis[...], grad[...], ((1,), (0,)))
    rot_other = dot(basis[...], other[...], ((1,), (0,)))
    rot[...] = rot_own
    both = jnp.concatenate([rot_own, rot_other], 1).astype(jnp.bfloat16)
    quarter = sent.shape[0]
    for at, size in cuts(grad.shape[0], 768):
        part = pl.ds(at, size)
        rows = jnp.concatenate([grad_rows[:, part], other_rows[:, part]], 0)
        product = dot(both, rows, ((1,), (0,)))
        kept[:, part] = product[: 2 * quarter]
        sent[:, part] = product[2 * quarter : 3 * quarter].astype(jnp.bfloat16)
        passed[:, part] = product[3 * quarter :].astype(jnp.bfloat16)


def power_products(pieces, grads):
    depth, rows = grads[0].shape
    count = sum(piece.shape[0] for piece in pieces)
    return pl.pallas_call(
        power_kernel,
        in_specs=[INSIDE] * (len(pieces) + len(grads)),
        out_specs=[INSIDE] * 5,
        out_shape=[
            pltpu.VMEM((count, depth), jnp.bfloat16),
            pltpu.VMEM((count, rows), jnp.float32),
            pltpu.VMEM((count // 2, depth), jnp.float32),
            pltpu.VMEM((count // 4, depth), jnp.bfloat16),
            pltpu.VMEM((count // 4, depth), jnp.bfloat16),
        ],
        compiler_params=PARAMS,
        name="power",
    )(*map(inside, (*pieces, *grads)))


def normal_kernel(kept, come, out):
    power = kept[...] + come[...].astype(jnp.float32)
    square = jnp.mean(power * power, axis=1, keepdims=True)
    out[...] = power / jnp.sqrt(square + 1e-06)


def normalised(kept, come):
    return pl.pallas_call(
        normal_kernel,
        in_specs=[INSIDE] * 2,
        out_specs=INSIDE,
        out_shape=jax.ShapeDtypeStruct(kept.shape, kept.dtype),
        compiler_params=PARAMS,
        name="normalise",
    )(inside(kept), inside(come))


def scale_kernel(
    orders, own, basis, grad, moment, rot_half, second, scaled, second_next, stored, rot, mom, sem
):
    copy = pltpu.make_async_copy(moment, stored, sem)
    copy.start()
    me = lax.axis_index("rows")
    core, chip = me & 1, me >> 1
    bits = len(orders[0])
    parity = functools.reduce(lambda a, b: a ^ b, [(me >> b) & 1 for b in range(bits + 1)])
    count = rot_half.shape[0]
    rot[:count] = rot_half[...]
    rot[count:] = dot(basis[count:], grad[...], ((1,), (0,)))
    mom[...] = dot(basis[...], moment[...], ((1,), (0,)))

    def place(offset, order):
        return sum(((offset >> bit) & 1) << step for step, bit in enumerate(order)) * own

    for half in range(2):

        @pl.when(parity == half)
        def _():
            for offset in range(1 << bits):
                mine = pl.ds(place(offset, orders[half]), own)
                theirs = pl.ds(count + place(offset, orders[1 - half]), own)
                first = core == odd(offset)
                tile = pl.ds(pl.multiple_of((chip ^ offset) * 2 * own, 2 * own), 2 * own)

                def joined(ref):
                    a, b = ref[mine], ref[theirs]
                    return jnp.where(
                        first, jnp.concatenate([a, b], 0), jnp.concatenate([b, a], 0)
                    )

                turned = joined(rot)
                value = 0.95 * second[tile] + 0.05 * turned * turned
                second_next[tile] = value
                ratio = joined(mom) / (jnp.sqrt(value) + 1e-08)
                rot[mine] = jnp.where(first, ratio[:own], ratio[own:])
                rot[theirs] = jnp.where(first, ratio[own:], ratio[:own])

    scaled[...] = rot[...].astype(jnp.bfloat16)
    copy.wait()


def scaled_rotation(orders, own, basis, grad, moment, rot_half, second):
    count, rows = basis.shape[0], grad.shape[1]
    return pl.pallas_call(
        functools.partial(scale_kernel, orders, own),
        in_specs=[INSIDE] * 5,
        out_specs=[INSIDE, INSIDE, ANYWHERE],
        out_shape=[
            pltpu.VMEM((count, rows), jnp.bfloat16),
            jax.ShapeDtypeStruct((count, rows), jnp.float32),
            jax.ShapeDtypeStruct(moment.shape, moment.dtype),
        ],
        scratch_shapes=[pltpu.VMEM((count, rows), jnp.float32)] * 2 + [pltpu.SemaphoreType.DMA],
        compiler_params=PARAMS,
        name="scale",
    )(*map(inside, (basis, grad, moment, rot_half, second)))


def update_kernel(basis, scaled, out, held, sems):
    copies = []
    for i, (at, size) in enumerate(cuts(out.shape[0], 640)):
        part = pl.ds(at, size)
        held[part] = dot(basis[:, part], scaled[...], ((0,), (0,))).astype(jnp.bfloat16)
        copy = pltpu.make_async_copy(held.at[part], out.at[part], sems.at[i])
        copy.start()
        copies.append(copy)
    for copy in copies:
        copy.wait()


def new_update(basis, scaled):
    depth, rows = basis.shape[1], scaled.shape[1]
    return pl.pallas_call(
        update_kernel,
        in_specs=[INSIDE] * 2,
        out_specs=ANYWHERE,
        out_shape=jax.ShapeDtypeStruct((depth, rows), jnp.bfloat16),
        scratch_shapes=[
            pltpu.VMEM((depth, rows), jnp.bfloat16),
            pltpu.SemaphoreType.DMA((len(cuts(depth, 640)),)),
        ],
        compiler_params=PARAMS,
        name="update",
    )(inside(basis), inside(scaled))


def shards(n, grad, moment, second, basis):
    bits = n.bit_length() - 2
    own = basis.shape[0]
    far, near = (bits - 1,), tuple(reversed(range(bits - 1)))
    orders = (far + near, far + near[-1:] + near[:-1])

    def exchange(value, step):
        pairs = [(i, i ^ (2 << orders[odd(i)][step]) ^ 1) for i in range(n)]
        return lax.ppermute(value, "rows", pairs)

    def across(value):
        return lax.ppermute(value, "rows", [(i, i ^ 1) for i in range(n)])

    grad, moment, second = grad.T, moment.T, second.T

    come = exchange(basis, 0)
    grad, held = load(grad, basis)
    come, grad, held = tie(come, grad, held)
    other = across(grad)
    held = jnp.concatenate([held, come], 0)
    for step in range(1, bits - 2):
        held = jnp.concatenate([held, exchange(held, step)], 0)
    first = exchange(held, bits - 2)
    second_hand = exchange(held, bits - 1)
    first, grad = tie(first, grad)
    last = exchange(first, bits - 1)
    second_hand, grad, other = tie(second_hand, grad, other)
    grad_rows, other_rows = transposed(grad, other)
    last, grad_rows, other_rows = tie(last, grad_rows, other_rows)
    held, rot_half, kept, sent, passed = power_products(
        (held, first, second_hand, last), (grad, other, grad_rows, other_rows)
    )
    come = exchange(passed, bits - 1)
    moment, _ = tie(moment, sent)
    moment = new_moment(grad, moment)
    held, sent, moment = tie(held, sent, moment)
    come_last = exchange(sent, bits - 1)
    theirs = across(held)
    come, moment = tie(come, moment)
    quarter = sent.shape[0]
    turned = kept[quarter:] + come.astype(jnp.float32)
    come = exchange(turned.astype(jnp.bfloat16), bits - 2)
    come_last, theirs, _ = tie(come_last, theirs, turned)
    whole = jnp.concatenate([held, theirs], 0)
    scaled, second_next, moment_next = scaled_rotation(
        orders, own, whole, grad, moment, rot_half, second
    )
    come, scaled, second_next, moment_next = tie(come, scaled, second_next, moment_next)
    kept = kept[:quarter] + come_last.astype(jnp.float32)
    for step in reversed(range(bits - 2)):
        kept = kept + come.astype(jnp.float32)
        half = kept.shape[0] // 2
        come = exchange(kept[half:].astype(jnp.bfloat16), step)
        kept = kept[:half]
        if step == 0:
            scaled, kept = tie(scaled, kept)
            update = new_update(whole, scaled)
            come, update = tie(come, update)
    basis_next = normalised(kept, come)
    return update.T, moment_next.T, second_next.T, basis_next


def solution(mesh):
    n = mesh.shape["rows"]
    placed = P(("groups", "rows"), None)
    return jax.shard_map(
        lambda *arrays: shards(n, *arrays),
        mesh=mesh,
        in_specs=(placed,) * 4,
        out_specs=(placed,) * 4,
        check_vma=False,
    )
```

```python
import functools

import jax
import jax.numpy as jnp
from jax import lax
from jax.experimental import pallas as pl
from jax.experimental.pallas import tpu as pltpu
from jax.sharding import PartitionSpec as P

INSIDE = pl.BlockSpec(memory_space=pltpu.VMEM)
ANYWHERE = pl.BlockSpec(memory_space=pl.ANY)
PARAMS = pltpu.CompilerParams(vmem_limit_bytes=24 << 20)


def inside(value):
    return pltpu.with_memory_space_constraint(value, pltpu.VMEM)


def tie(*values):
    return lax.optimization_barrier(values)


def cuts(depth, size):
    return [(at, min(size, depth - at)) for at in range(0, depth, size)]


def odd(i):
    return i.bit_count() & 1


def dot(left, right, dims):
    return lax.dot_general(left, right, (dims, ((), ())), preferred_element_type=jnp.float32)


def start_copies(source, target, sems, size):
    copies = []
    for i, (at, rows) in enumerate(cuts(source.shape[0], size)):
        part = pl.ds(at, rows)
        copies.append(pltpu.make_async_copy(source.at[part], target.at[part], sems.at[i]))
        copies[-1].start()
    return copies


def load_kernel(grad, basis, grad_in, basis_in, sems, sem):
    last = pltpu.make_async_copy(basis, basis_in, sem)
    last.start()
    for copy in start_copies(grad, grad_in, sems, 720):
        copy.wait()
    last.wait()


def load(*values):
    out = pl.pallas_call(
        load_kernel,
        in_specs=[pl.BlockSpec(memory_space=pltpu.HBM)] * len(values),
        out_specs=[INSIDE] * len(values),
        out_shape=[pltpu.VMEM(value.shape, value.dtype) for value in values],
        scratch_shapes=[
            pltpu.SemaphoreType.DMA((len(cuts(values[0].shape[0], 720)),)),
            pltpu.SemaphoreType.DMA,
        ],
        compiler_params=PARAMS,
        name="load",
    )(*[pltpu.with_memory_space_constraint(value, pltpu.HBM) for value in values])
    return out


def moment_kernel(grad, moment, out):
    out[...] = (0.9 * moment[...].astype(jnp.float32) + 0.1 * grad[...].astype(jnp.float32)).astype(
        jnp.bfloat16
    )


def new_moment(grad, moment):
    return pl.pallas_call(
        moment_kernel,
        in_specs=[INSIDE, INSIDE],
        out_specs=INSIDE,
        out_shape=pltpu.VMEM(grad.shape, grad.dtype),
        compiler_params=PARAMS,
        name="moment",
    )(inside(grad), inside(moment))


def transpose_kernel(*refs):
    count = len(refs) // 2
    for value, out in zip(refs[:count], refs[count:]):
        out[...] = value[...].T


def transposed(*values):
    return pl.pallas_call(
        transpose_kernel,
        in_specs=[INSIDE] * len(values),
        out_specs=[INSIDE] * len(values),
        out_shape=[pltpu.VMEM(value.shape[::-1], value.dtype) for value in values],
        compiler_params=PARAMS,
        name="transpose",
    )(*map(inside, values))


def power_kernel(*refs):
    *pieces, grad, other, grad_rows, other_rows, basis, rot, kept, sent, passed = refs
    basis[...] = jnp.concatenate([piece[...] for piece in pieces], 0)
    rot_own = dot(basis[...], grad[...], ((1,), (0,)))
    rot_other = dot(basis[...], other[...], ((1,), (0,)))
    rot[...] = rot_own
    both = jnp.concatenate([rot_own, rot_other], 1).astype(jnp.bfloat16)
    quarter = sent.shape[0]
    for at, size in cuts(grad.shape[0], 768):
        part = pl.ds(at, size)
        rows = jnp.concatenate([grad_rows[:, part], other_rows[:, part]], 0)
        product = dot(both, rows, ((1,), (0,)))
        kept[:, part] = product[: 2 * quarter]
        sent[:, part] = product[2 * quarter : 3 * quarter].astype(jnp.bfloat16)
        passed[:, part] = product[3 * quarter :].astype(jnp.bfloat16)


def power_products(pieces, grads):
    depth, rows = grads[0].shape
    count = sum(piece.shape[0] for piece in pieces)
    return pl.pallas_call(
        power_kernel,
        in_specs=[INSIDE] * (len(pieces) + len(grads)),
        out_specs=[INSIDE] * 5,
        out_shape=[
            pltpu.VMEM((count, depth), jnp.bfloat16),
            pltpu.VMEM((count, rows), jnp.float32),
            pltpu.VMEM((count // 2, depth), jnp.float32),
            pltpu.VMEM((count // 4, depth), jnp.bfloat16),
            pltpu.VMEM((count // 4, depth), jnp.bfloat16),
        ],
        compiler_params=PARAMS,
        name="power",
    )(*map(inside, (*pieces, *grads)))


def normal_kernel(kept, come, out):
    power = kept[...] + come[...].astype(jnp.float32)
    square = jnp.mean(power * power, axis=1, keepdims=True)
    out[...] = power / jnp.sqrt(square + 1e-06)


def normalised(kept, come):
    return pl.pallas_call(
        normal_kernel,
        in_specs=[INSIDE] * 2,
        out_specs=INSIDE,
        out_shape=jax.ShapeDtypeStruct(kept.shape, kept.dtype),
        compiler_params=PARAMS,
        name="normalise",
    )(inside(kept), inside(come))


def scale_kernel(
    orders, own, basis, grad, moment, rot_half, second, scaled, second_next, stored, rot, mom, sems
):
    copies = start_copies(moment, stored, sems, 720)
    me = lax.axis_index("rows")
    core, chip = me & 1, me >> 1
    bits = len(orders[0])
    parity = functools.reduce(lambda a, b: a ^ b, [(me >> b) & 1 for b in range(bits + 1)])
    count = rot_half.shape[0]
    rot[:count] = rot_half[...]
    rot[count:] = dot(basis[count:], grad[...], ((1,), (0,)))
    mom[...] = dot(basis[...], moment[...], ((1,), (0,)))

    def place(offset, order):
        return sum(((offset >> bit) & 1) << step for step, bit in enumerate(order)) * own

    for half in range(2):

        @pl.when(parity == half)
        def _():
            for offset in range(1 << bits):
                mine = pl.ds(place(offset, orders[half]), own)
                theirs = pl.ds(count + place(offset, orders[1 - half]), own)
                first = core == odd(offset)
                tile = pl.ds(pl.multiple_of((chip ^ offset) * 2 * own, 2 * own), 2 * own)

                def joined(ref):
                    a, b = ref[mine], ref[theirs]
                    return jnp.where(
                        first, jnp.concatenate([a, b], 0), jnp.concatenate([b, a], 0)
                    )

                turned = joined(rot)
                value = 0.95 * second[tile] + 0.05 * turned * turned
                second_next[tile] = value
                ratio = joined(mom) / (jnp.sqrt(value) + 1e-08)
                rot[mine] = jnp.where(first, ratio[:own], ratio[own:])
                rot[theirs] = jnp.where(first, ratio[own:], ratio[:own])

    scaled[...] = rot[...].astype(jnp.bfloat16)
    for copy in copies:
        copy.wait()


def scaled_rotation(orders, own, basis, grad, moment, rot_half, second):
    count, rows = basis.shape[0], grad.shape[1]
    return pl.pallas_call(
        functools.partial(scale_kernel, orders, own),
        in_specs=[INSIDE] * 5,
        out_specs=[INSIDE, INSIDE, ANYWHERE],
        out_shape=[
            pltpu.VMEM((count, rows), jnp.bfloat16),
            jax.ShapeDtypeStruct((count, rows), jnp.float32),
            jax.ShapeDtypeStruct(moment.shape, moment.dtype),
        ],
        scratch_shapes=[
            pltpu.VMEM((count, rows), jnp.float32),
            pltpu.VMEM((count, rows), jnp.float32),
            pltpu.SemaphoreType.DMA((len(cuts(moment.shape[0], 720)),)),
        ],
        compiler_params=PARAMS,
        name="scale",
    )(*map(inside, (basis, grad, moment, rot_half, second)))


def update_kernel(basis, scaled, out, held, sems):
    copies = []
    for i, (at, size) in enumerate(cuts(out.shape[0], 640)):
        part = pl.ds(at, size)
        held[part] = dot(basis[:, part], scaled[...], ((0,), (0,))).astype(jnp.bfloat16)
        copy = pltpu.make_async_copy(held.at[part], out.at[part], sems.at[i])
        copy.start()
        copies.append(copy)
    for copy in copies:
        copy.wait()


def new_update(basis, scaled):
    depth, rows = basis.shape[1], scaled.shape[1]
    return pl.pallas_call(
        update_kernel,
        in_specs=[INSIDE] * 2,
        out_specs=ANYWHERE,
        out_shape=jax.ShapeDtypeStruct((depth, rows), jnp.bfloat16),
        scratch_shapes=[
            pltpu.VMEM((depth, rows), jnp.bfloat16),
            pltpu.SemaphoreType.DMA((len(cuts(depth, 640)),)),
        ],
        compiler_params=PARAMS,
        name="update",
    )(inside(basis), inside(scaled))


def shards(n, grad, moment, second, basis):
    bits = n.bit_length() - 2
    own = basis.shape[0]
    far, near = (bits - 1,), tuple(reversed(range(bits - 1)))
    orders = (far + near, far + near[-1:] + near[:-1])

    def exchange(value, step):
        pairs = [(i, i ^ (2 << orders[odd(i)][step]) ^ 1) for i in range(n)]
        return lax.ppermute(value, "rows", pairs)

    def across(value):
        return lax.ppermute(value, "rows", [(i, i ^ 1) for i in range(n)])

    grad, moment, second = grad.T, moment.T, second.T

    come = exchange(basis, 0)
    grad, held = load(grad, basis)
    come, grad, held = tie(come, grad, held)
    other = across(grad)
    held = jnp.concatenate([held, come], 0)
    for step in range(1, bits - 2):
        held = jnp.concatenate([held, exchange(held, step)], 0)
    first = exchange(held, bits - 2)
    second_hand = exchange(held, bits - 1)
    first, grad = tie(first, grad)
    last = exchange(first, bits - 1)
    second_hand, grad, other = tie(second_hand, grad, other)
    grad_rows, other_rows = transposed(grad, other)
    last, grad_rows, other_rows = tie(last, grad_rows, other_rows)
    held, rot_half, kept, sent, passed = power_products(
        (held, first, second_hand, last), (grad, other, grad_rows, other_rows)
    )
    come = exchange(passed, bits - 1)
    moment, _ = tie(moment, sent)
    moment = new_moment(grad, moment)
    held, sent, moment = tie(held, sent, moment)
    come_last = exchange(sent, bits - 1)
    theirs = across(held)
    come, moment = tie(come, moment)
    quarter = sent.shape[0]
    turned = kept[quarter:] + come.astype(jnp.float32)
    come = exchange(turned.astype(jnp.bfloat16), bits - 2)
    theirs, _ = tie(theirs, turned)
    whole = jnp.concatenate([held, theirs], 0)
    scaled, second_next, moment_next = scaled_rotation(
        orders, own, whole, grad, moment, rot_half, second
    )
    come, scaled, second_next, moment_next = tie(come, scaled, second_next, moment_next)
    kept = kept[:quarter] + come_last.astype(jnp.float32)
    for step in reversed(range(bits - 2)):
        kept = kept + come.astype(jnp.float32)
        half = kept.shape[0] // 2
        come = exchange(kept[half:].astype(jnp.bfloat16), step)
        kept = kept[:half]
        if step == 0:
            scaled, kept = tie(scaled, kept)
            update = new_update(whole, scaled)
            come, update = tie(come, update)
    basis_next = normalised(kept, come)
    return update.T, moment_next.T, second_next.T, basis_next


def solution(mesh):
    n = mesh.shape["rows"]
    placed = P(("groups", "rows"), None)
    return jax.shard_map(
        lambda *arrays: shards(n, *arrays),
        mesh=mesh,
        in_specs=(placed,) * 4,
        out_specs=(placed,) * 4,
        check_vma=False,
    )
```

```python
import functools

import jax
import jax.numpy as jnp
from jax import lax
from jax.experimental import pallas as pl
from jax.experimental.pallas import tpu as pltpu
from jax.sharding import PartitionSpec as P

INSIDE = pl.BlockSpec(memory_space=pltpu.VMEM)
ANYWHERE = pl.BlockSpec(memory_space=pl.ANY)
PARAMS = pltpu.CompilerParams(vmem_limit_bytes=24 << 20)


def inside(value):
    return pltpu.with_memory_space_constraint(value, pltpu.VMEM)


def tie(*values):
    return lax.optimization_barrier(values)


def cuts(depth, size):
    return [(at, min(size, depth - at)) for at in range(0, depth, size)]


def odd(i):
    return i.bit_count() & 1


def dot(left, right, dims):
    return lax.dot_general(left, right, (dims, ((), ())), preferred_element_type=jnp.float32)


def start_copies(source, target, sems, size):
    copies = []
    for i, (at, rows) in enumerate(cuts(source.shape[0], size)):
        part = pl.ds(at, rows)
        copies.append(pltpu.make_async_copy(source.at[part], target.at[part], sems.at[i]))
        copies[-1].start()
    return copies


def load_kernel(grad, basis, grad_in, basis_in, sems, sem):
    last = pltpu.make_async_copy(basis, basis_in, sem)
    last.start()
    for copy in start_copies(grad, grad_in, sems, 720):
        copy.wait()
    last.wait()


def load(*values):
    out = pl.pallas_call(
        load_kernel,
        in_specs=[pl.BlockSpec(memory_space=pltpu.HBM)] * len(values),
        out_specs=[INSIDE] * len(values),
        out_shape=[pltpu.VMEM(value.shape, value.dtype) for value in values],
        scratch_shapes=[
            pltpu.SemaphoreType.DMA((len(cuts(values[0].shape[0], 720)),)),
            pltpu.SemaphoreType.DMA,
        ],
        compiler_params=PARAMS,
        name="load",
    )(*[pltpu.with_memory_space_constraint(value, pltpu.HBM) for value in values])
    return out


def moment_kernel(grad, moment, held, stored, sems):
    copies = []
    for i, (at, size) in enumerate(cuts(grad.shape[0], 960)):
        part = pl.ds(at, size)
        held[part] = (
            0.9 * moment[part].astype(jnp.float32) + 0.1 * grad[part].astype(jnp.float32)
        ).astype(jnp.bfloat16)
        copy = pltpu.make_async_copy(held.at[part], stored.at[part], sems.at[i])
        copy.start()
        copies.append(copy)
    for copy in copies:
        copy.wait()


def new_moment(grad, moment):
    return pl.pallas_call(
        moment_kernel,
        in_specs=[INSIDE, INSIDE],
        out_specs=[INSIDE, ANYWHERE],
        out_shape=[
            pltpu.VMEM(grad.shape, grad.dtype),
            jax.ShapeDtypeStruct(grad.shape, grad.dtype),
        ],
        scratch_shapes=[pltpu.SemaphoreType.DMA((len(cuts(grad.shape[0], 960)),))],
        compiler_params=PARAMS,
        name="moment",
    )(inside(grad), inside(moment))


def transpose_kernel(*refs):
    count = len(refs) // 2
    for value, out in zip(refs[:count], refs[count:]):
        out[...] = value[...].T


def transposed(*values):
    return pl.pallas_call(
        transpose_kernel,
        in_specs=[INSIDE] * len(values),
        out_specs=[INSIDE] * len(values),
        out_shape=[pltpu.VMEM(value.shape[::-1], value.dtype) for value in values],
        compiler_params=PARAMS,
        name="transpose",
    )(*map(inside, values))


def power_kernel(*refs):
    *pieces, grad, other, grad_rows, other_rows, basis, rot, kept, sent, passed = refs
    basis[...] = jnp.concatenate([piece[...] for piece in pieces], 0)
    rot_own = dot(basis[...], grad[...], ((1,), (0,)))
    rot_other = dot(basis[...], other[...], ((1,), (0,)))
    rot[...] = rot_own
    both = jnp.concatenate([rot_own, rot_other], 1).astype(jnp.bfloat16)
    quarter = sent.shape[0]
    for at, size in cuts(grad.shape[0], 768):
        part = pl.ds(at, size)
        rows = jnp.concatenate([grad_rows[:, part], other_rows[:, part]], 0)
        product = dot(both, rows, ((1,), (0,)))
        kept[:, part] = product[: 2 * quarter]
        sent[:, part] = product[2 * quarter : 3 * quarter].astype(jnp.bfloat16)
        passed[:, part] = product[3 * quarter :].astype(jnp.bfloat16)


def power_products(pieces, grads):
    depth, rows = grads[0].shape
    count = sum(piece.shape[0] for piece in pieces)
    return pl.pallas_call(
        power_kernel,
        in_specs=[INSIDE] * (len(pieces) + len(grads)),
        out_specs=[INSIDE] * 5,
        out_shape=[
            pltpu.VMEM((count, depth), jnp.bfloat16),
            pltpu.VMEM((count, rows), jnp.float32),
            pltpu.VMEM((count // 2, depth), jnp.float32),
            pltpu.VMEM((count // 4, depth), jnp.bfloat16),
            pltpu.VMEM((count // 4, depth), jnp.bfloat16),
        ],
        compiler_params=PARAMS,
        name="power",
    )(*map(inside, (*pieces, *grads)))


def normal_kernel(kept, come, out):
    power = kept[...] + come[...].astype(jnp.float32)
    square = jnp.mean(power * power, axis=1, keepdims=True)
    out[...] = power / jnp.sqrt(square + 1e-06)


def normalised(kept, come):
    return pl.pallas_call(
        normal_kernel,
        in_specs=[INSIDE] * 2,
        out_specs=INSIDE,
        out_shape=jax.ShapeDtypeStruct(kept.shape, kept.dtype),
        compiler_params=PARAMS,
        name="normalise",
    )(inside(kept), inside(come))


def scale_kernel(
    orders, own, basis, grad, moment, rot_half, second, scaled, second_next, rot, mom
):
    me = lax.axis_index("rows")
    core, chip = me & 1, me >> 1
    bits = len(orders[0])
    parity = functools.reduce(lambda a, b: a ^ b, [(me >> b) & 1 for b in range(bits + 1)])
    count = rot_half.shape[0]
    rot[:count] = rot_half[...]
    rot[count:] = dot(basis[count:], grad[...], ((1,), (0,)))
    mom[...] = dot(basis[...], moment[...], ((1,), (0,)))

    def place(offset, order):
        return sum(((offset >> bit) & 1) << step for step, bit in enumerate(order)) * own

    for half in range(2):

        @pl.when(parity == half)
        def _():
            for offset in range(1 << bits):
                mine = pl.ds(place(offset, orders[half]), own)
                theirs = pl.ds(count + place(offset, orders[1 - half]), own)
                first = core == odd(offset)
                tile = pl.ds(pl.multiple_of((chip ^ offset) * 2 * own, 2 * own), 2 * own)

                def joined(ref):
                    a, b = ref[mine], ref[theirs]
                    return jnp.where(
                        first, jnp.concatenate([a, b], 0), jnp.concatenate([b, a], 0)
                    )

                turned = joined(rot)
                value = 0.95 * second[tile] + 0.05 * turned * turned
                second_next[tile] = value
                ratio = joined(mom) / (jnp.sqrt(value) + 1e-08)
                rot[mine] = jnp.where(first, ratio[:own], ratio[own:])
                rot[theirs] = jnp.where(first, ratio[own:], ratio[:own])

    scaled[...] = rot[...].astype(jnp.bfloat16)


def scaled_rotation(orders, own, basis, grad, moment, rot_half, second):
    count, rows = basis.shape[0], grad.shape[1]
    return pl.pallas_call(
        functools.partial(scale_kernel, orders, own),
        in_specs=[INSIDE] * 5,
        out_specs=[INSIDE, INSIDE],
        out_shape=[
            pltpu.VMEM((count, rows), jnp.bfloat16),
            jax.ShapeDtypeStruct((count, rows), jnp.float32),
        ],
        scratch_shapes=[pltpu.VMEM((count, rows), jnp.float32)] * 2,
        compiler_params=PARAMS,
        name="scale",
    )(*map(inside, (basis, grad, moment, rot_half, second)))


def update_kernel(basis, scaled, out, held, sems):
    copies = []
    for i, (at, size) in enumerate(cuts(out.shape[0], 640)):
        part = pl.ds(at, size)
        held[part] = dot(basis[:, part], scaled[...], ((0,), (0,))).astype(jnp.bfloat16)
        copy = pltpu.make_async_copy(held.at[part], out.at[part], sems.at[i])
        copy.start()
        copies.append(copy)
    for copy in copies:
        copy.wait()


def new_update(basis, scaled):
    depth, rows = basis.shape[1], scaled.shape[1]
    return pl.pallas_call(
        update_kernel,
        in_specs=[INSIDE] * 2,
        out_specs=ANYWHERE,
        out_shape=jax.ShapeDtypeStruct((depth, rows), jnp.bfloat16),
        scratch_shapes=[
            pltpu.VMEM((depth, rows), jnp.bfloat16),
            pltpu.SemaphoreType.DMA((len(cuts(depth, 640)),)),
        ],
        compiler_params=PARAMS,
        name="update",
    )(inside(basis), inside(scaled))


def shards(n, grad, moment, second, basis):
    bits = n.bit_length() - 2
    own = basis.shape[0]
    far, near = (bits - 1,), tuple(reversed(range(bits - 1)))
    orders = (far + near, far + near[-1:] + near[:-1])

    def exchange(value, step):
        pairs = [(i, i ^ (2 << orders[odd(i)][step]) ^ 1) for i in range(n)]
        return lax.ppermute(value, "rows", pairs)

    def across(value):
        return lax.ppermute(value, "rows", [(i, i ^ 1) for i in range(n)])

    grad, moment, second = grad.T, moment.T, second.T

    come = exchange(basis, 0)
    grad, held = load(grad, basis)
    come, grad, held = tie(come, grad, held)
    other = across(grad)
    held = jnp.concatenate([held, come], 0)
    for step in range(1, bits - 2):
        held = jnp.concatenate([held, exchange(held, step)], 0)
    first = exchange(held, bits - 2)
    second_hand = exchange(held, bits - 1)
    first, grad = tie(first, grad)
    last = exchange(first, bits - 1)
    second_hand, grad, other = tie(second_hand, grad, other)
    grad_rows, other_rows = transposed(grad, other)
    last, grad_rows, other_rows = tie(last, grad_rows, other_rows)
    held, rot_half, kept, sent, passed = power_products(
        (held, first, second_hand, last), (grad, other, grad_rows, other_rows)
    )
    come = exchange(passed, bits - 1)
    moment, _ = tie(moment, sent)
    moment, moment_next = new_moment(grad, moment)
    held, sent, moment, moment_next = tie(held, sent, moment, moment_next)
    come_last = exchange(sent, bits - 1)
    theirs = across(held)
    come, moment = tie(come, moment)
    quarter = sent.shape[0]
    turned = kept[quarter:] + come.astype(jnp.float32)
    come = exchange(turned.astype(jnp.bfloat16), bits - 2)
    theirs, _ = tie(theirs, turned)
    whole = jnp.concatenate([held, theirs], 0)
    scaled, second_next = scaled_rotation(
        orders, own, whole, grad, moment, rot_half, second
    )
    come, scaled, second_next = tie(come, scaled, second_next)
    kept = kept[:quarter] + come_last.astype(jnp.float32)
    for step in reversed(range(bits - 2)):
        kept = kept + come.astype(jnp.float32)
        half = kept.shape[0] // 2
        come = exchange(kept[half:].astype(jnp.bfloat16), step)
        kept = kept[:half]
        if step == 0:
            scaled, kept = tie(scaled, kept)
            update = new_update(whole, scaled)
            come, update = tie(come, update)
    basis_next = normalised(kept, come)
    return update.T, moment_next.T, second_next.T, basis_next


def solution(mesh):
    n = mesh.shape["rows"]
    placed = P(("groups", "rows"), None)
    return jax.shard_map(
        lambda *arrays: shards(n, *arrays),
        mesh=mesh,
        in_specs=(placed,) * 4,
        out_specs=(placed,) * 4,
        check_vma=False,
    )
```

```python
import functools

import jax
import jax.numpy as jnp
from jax import lax
from jax.experimental import pallas as pl
from jax.experimental.pallas import tpu as pltpu
from jax.sharding import PartitionSpec as P

INSIDE = pl.BlockSpec(memory_space=pltpu.VMEM)
ANYWHERE = pl.BlockSpec(memory_space=pl.ANY)
PARAMS = pltpu.CompilerParams(vmem_limit_bytes=24 << 20)


def inside(value):
    return pltpu.with_memory_space_constraint(value, pltpu.VMEM)


def tie(*values):
    return lax.optimization_barrier(values)


def cuts(depth, size):
    return [(at, min(size, depth - at)) for at in range(0, depth, size)]


def odd(i):
    return i.bit_count() & 1


def dot(left, right, dims):
    return lax.dot_general(left, right, (dims, ((), ())), preferred_element_type=jnp.float32)


def load_kernel(*refs):
    count = len(refs) // 2
    sems = refs[-1]
    copies = [
        pltpu.make_async_copy(refs[i], refs[count + i], sems.at[i]) for i in range(count)
    ]
    for copy in copies:
        copy.start()
    for copy in copies:
        copy.wait()


def load(*values):
    out = pl.pallas_call(
        load_kernel,
        in_specs=[pl.BlockSpec(memory_space=pltpu.HBM)] * len(values),
        out_specs=[INSIDE] * len(values),
        out_shape=[pltpu.VMEM(value.shape, value.dtype) for value in values],
        scratch_shapes=[pltpu.SemaphoreType.DMA((len(values),))],
        compiler_params=PARAMS,
        name="load",
    )(*[pltpu.with_memory_space_constraint(value, pltpu.HBM) for value in values])
    return out


def moment_kernel(begin, grad, moment, *refs):
    held, stored, sems = refs[-3:]
    copies = []
    for i, (at, size) in enumerate(cuts(grad.shape[0] // 2, 720)):
        part = pl.ds(begin + at, size)
        held[part] = (
            0.9 * moment[part].astype(jnp.float32) + 0.1 * grad[part].astype(jnp.float32)
        ).astype(jnp.bfloat16)
        copy = pltpu.make_async_copy(held.at[part], stored.at[part], sems.at[i])
        copy.start()
        copies.append(copy)
    for copy in copies:
        copy.wait()


def half_moment(grad, moment, *so_far):
    more = len(so_far) > 0
    half = grad.shape[0] // 2
    values = [inside(grad), inside(moment)]
    if more:
        values += [inside(so_far[0]), so_far[1]]
    return pl.pallas_call(
        functools.partial(moment_kernel, half if more else 0),
        in_specs=[INSIDE, INSIDE] + [INSIDE, ANYWHERE] * more,
        out_specs=[INSIDE, ANYWHERE],
        out_shape=[
            pltpu.VMEM(grad.shape, grad.dtype),
            jax.ShapeDtypeStruct(grad.shape, grad.dtype),
        ],
        input_output_aliases={2: 0, 3: 1} if more else {},
        scratch_shapes=[pltpu.SemaphoreType.DMA((len(cuts(half, 720)),))],
        compiler_params=PARAMS,
        name="moment",
    )(*values)


def transpose_kernel(*refs):
    count = len(refs) // 2
    for value, out in zip(refs[:count], refs[count:]):
        out[...] = value[...].T


def transposed(*values):
    return pl.pallas_call(
        transpose_kernel,
        in_specs=[INSIDE] * len(values),
        out_specs=[INSIDE] * len(values),
        out_shape=[pltpu.VMEM(value.shape[::-1], value.dtype) for value in values],
        compiler_params=PARAMS,
        name="transpose",
    )(*map(inside, values))


def power_kernel(*refs):
    *pieces, grad, other, grad_rows, other_rows, basis, rot, kept, sent = refs
    basis[...] = jnp.concatenate([piece[...] for piece in pieces], 0)
    rot_own = dot(basis[...], grad[...], ((1,), (0,)))
    rot_other = dot(basis[...], other[...], ((1,), (0,)))
    rot[...] = rot_own
    both = jnp.concatenate([rot_own, rot_other], 1).astype(jnp.bfloat16)
    half = kept.shape[0]
    for at, size in cuts(grad.shape[0], 768):
        part = pl.ds(at, size)
        rows = jnp.concatenate([grad_rows[:, part], other_rows[:, part]], 0)
        product = dot(both, rows, ((1,), (0,)))
        kept[:, part] = product[:half]
        sent[:, part] = product[half:].astype(jnp.bfloat16)


def power_products(pieces, grads):
    depth, rows = grads[0].shape
    count = sum(piece.shape[0] for piece in pieces)
    return pl.pallas_call(
        power_kernel,
        in_specs=[INSIDE] * (len(pieces) + len(grads)),
        out_specs=[INSIDE] * 4,
        out_shape=[
            pltpu.VMEM((count, depth), jnp.bfloat16),
            pltpu.VMEM((count, rows), jnp.float32),
            pltpu.VMEM((count // 2, depth), jnp.float32),
            pltpu.VMEM((count // 2, depth), jnp.bfloat16),
        ],
        compiler_params=PARAMS,
        name="power",
    )(*map(inside, (*pieces, *grads)))


def normal_kernel(kept, come, out):
    power = kept[...] + come[...].astype(jnp.float32)
    square = jnp.mean(power * power, axis=1, keepdims=True)
    out[...] = power / jnp.sqrt(square + 1e-06)


def normalised(kept, come):
    return pl.pallas_call(
        normal_kernel,
        in_specs=[INSIDE] * 2,
        out_specs=INSIDE,
        out_shape=jax.ShapeDtypeStruct(kept.shape, kept.dtype),
        compiler_params=PARAMS,
        name="normalise",
    )(inside(kept), inside(come))


def scale_kernel(orders, own, basis, grad, moment, rot_half, second, scaled, second_next, rot, mom):
    me = lax.axis_index("rows")
    core, chip = me & 1, me >> 1
    bits = len(orders[0])
    parity = functools.reduce(lambda a, b: a ^ b, [(me >> b) & 1 for b in range(bits + 1)])
    count = rot_half.shape[0]
    rot[:count] = rot_half[...]
    rot[count:] = dot(basis[count:], grad[...], ((1,), (0,)))
    mom[...] = dot(basis[...], moment[...], ((1,), (0,)))

    def place(offset, order):
        return sum(((offset >> bit) & 1) << step for step, bit in enumerate(order)) * own

    for half in range(2):

        @pl.when(parity == half)
        def _():
            for offset in range(1 << bits):
                mine = pl.ds(place(offset, orders[half]), own)
                theirs = pl.ds(count + place(offset, orders[1 - half]), own)
                first = core == odd(offset)
                tile = pl.ds(pl.multiple_of((chip ^ offset) * 2 * own, 2 * own), 2 * own)

                def joined(ref):
                    a, b = ref[mine], ref[theirs]
                    return jnp.where(
                        first, jnp.concatenate([a, b], 0), jnp.concatenate([b, a], 0)
                    )

                turned = joined(rot)
                value = 0.95 * second[tile] + 0.05 * turned * turned
                second_next[tile] = value
                ratio = joined(mom) / (jnp.sqrt(value) + 1e-08)
                rot[mine] = jnp.where(first, ratio[:own], ratio[own:])
                rot[theirs] = jnp.where(first, ratio[own:], ratio[:own])

    scaled[...] = rot[...].astype(jnp.bfloat16)


def scaled_rotation(orders, own, basis, grad, moment, rot_half, second):
    count, rows = basis.shape[0], grad.shape[1]
    return pl.pallas_call(
        functools.partial(scale_kernel, orders, own),
        in_specs=[INSIDE] * 5,
        out_specs=[INSIDE] * 2,
        out_shape=[
            pltpu.VMEM((count, rows), jnp.bfloat16),
            jax.ShapeDtypeStruct((count, rows), jnp.float32),
        ],
        scratch_shapes=[pltpu.VMEM((count, rows), jnp.float32)] * 2,
        compiler_params=PARAMS,
        name="scale",
    )(*map(inside, (basis, grad, moment, rot_half, second)))


def update_kernel(basis, scaled, out, held, sems):
    copies = []
    for i, (at, size) in enumerate(cuts(out.shape[0], 640)):
        part = pl.ds(at, size)
        held[part] = dot(basis[:, part], scaled[...], ((0,), (0,))).astype(jnp.bfloat16)
        copy = pltpu.make_async_copy(held.at[part], out.at[part], sems.at[i])
        copy.start()
        copies.append(copy)
    for copy in copies:
        copy.wait()


def new_update(basis, scaled):
    depth, rows = basis.shape[1], scaled.shape[1]
    return pl.pallas_call(
        update_kernel,
        in_specs=[INSIDE] * 2,
        out_specs=ANYWHERE,
        out_shape=jax.ShapeDtypeStruct((depth, rows), jnp.bfloat16),
        scratch_shapes=[
            pltpu.VMEM((depth, rows), jnp.bfloat16),
            pltpu.SemaphoreType.DMA((len(cuts(depth, 640)),)),
        ],
        compiler_params=PARAMS,
        name="update",
    )(inside(basis), inside(scaled))


def shards(n, grad, moment, second, basis):
    bits = n.bit_length() - 2
    own = basis.shape[0]
    far, near = (bits - 1,), tuple(reversed(range(bits - 1)))
    orders = (far + near, far + near[-1:] + near[:-1])

    def exchange(value, step):
        pairs = [(i, i ^ (2 << orders[odd(i)][step]) ^ 1) for i in range(n)]
        return lax.ppermute(value, "rows", pairs)

    def across(value):
        return lax.ppermute(value, "rows", [(i, i ^ 1) for i in range(n)])

    grad, moment, second = grad.T, moment.T, second.T

    come = exchange(basis, 0)
    grad, held = load(grad, basis)
    come, grad, held = tie(come, grad, held)
    other = across(grad)
    held = jnp.concatenate([held, come], 0)
    for step in range(1, bits - 2):
        held = jnp.concatenate([held, exchange(held, step)], 0)
    first = exchange(held, bits - 2)
    second_hand = exchange(held, bits - 1)
    first, grad = tie(first, grad)
    last = exchange(first, bits - 1)
    second_hand, grad, other = tie(second_hand, grad, other)
    grad_rows, other_rows = transposed(grad, other)
    last, grad_rows, other_rows = tie(last, grad_rows, other_rows)
    held, rot_half, kept, sent = power_products(
        (held, first, second_hand, last), (grad, other, grad_rows, other_rows)
    )
    come = exchange(sent, bits - 1)
    moment, _ = tie(moment, sent)
    first_half = half_moment(grad, moment)
    held, *first_half = tie(held, *first_half)
    theirs = across(held)
    moment_in, moment_next = half_moment(grad, moment, *first_half)
    come, moment_in, moment_next = tie(come, moment_in, moment_next)
    for step in reversed(range(bits)):
        if step == 0:
            break
        kept = kept + come.astype(jnp.float32)
        half = kept.shape[0] // 2
        come = exchange(kept[half:].astype(jnp.bfloat16), step - 1)
        kept = kept[:half]
        if step == bits - 1:
            theirs, kept = tie(theirs, kept)
            whole = jnp.concatenate([held, theirs], 0)
            scaled, second_next = scaled_rotation(
                orders, own, whole, grad, moment_in, rot_half, second
            )
            come, scaled, second_next = tie(come, scaled, second_next)
        if step == bits - 2:
            scaled, kept = tie(scaled, kept)
            update = new_update(whole, scaled)
            come, update = tie(come, update)
    basis_next = normalised(kept, come)
    return update.T, moment_next.T, second_next.T, basis_next


def solution(mesh):
    n = mesh.shape["rows"]
    placed = P(("groups", "rows"), None)
    return jax.shard_map(
        lambda *arrays: shards(n, *arrays),
        mesh=mesh,
        in_specs=(placed,) * 4,
        out_specs=(placed,) * 4,
        check_vma=False,
    )
```

```python
import functools

import jax
import jax.numpy as jnp
from jax import lax
from jax.experimental import pallas as pl
from jax.experimental.pallas import tpu as pltpu
from jax.sharding import PartitionSpec as P

INSIDE = pl.BlockSpec(memory_space=pltpu.VMEM)
ANYWHERE = pl.BlockSpec(memory_space=pl.ANY)
PARAMS = pltpu.CompilerParams(vmem_limit_bytes=24 << 20)


def inside(value):
    return pltpu.with_memory_space_constraint(value, pltpu.VMEM)


def tie(*values):
    return lax.optimization_barrier(values)


def cuts(depth, size):
    return [(at, min(size, depth - at)) for at in range(0, depth, size)]


def odd(i):
    return i.bit_count() & 1


def dot(left, right, dims):
    return lax.dot_general(left, right, (dims, ((), ())), preferred_element_type=jnp.float32)


def load_kernel(*refs):
    count = len(refs) // 2
    sems = refs[-1]
    copies = [
        pltpu.make_async_copy(refs[i], refs[count + i], sems.at[i]) for i in range(count)
    ]
    for copy in copies:
        copy.start()
    for copy in copies:
        copy.wait()


def load(*values):
    out = pl.pallas_call(
        load_kernel,
        in_specs=[pl.BlockSpec(memory_space=pltpu.HBM)] * len(values),
        out_specs=[INSIDE] * len(values),
        out_shape=[pltpu.VMEM(value.shape, value.dtype) for value in values],
        scratch_shapes=[pltpu.SemaphoreType.DMA((len(values),))],
        compiler_params=PARAMS,
        name="load",
    )(*[pltpu.with_memory_space_constraint(value, pltpu.HBM) for value in values])
    return out


def moment_kernel(grad, moment, held, stored, sems):
    copies = []
    for i, (at, size) in enumerate(cuts(grad.shape[0], 960)):
        part = pl.ds(at, size)
        held[part] = (
            0.9 * moment[part].astype(jnp.float32) + 0.1 * grad[part].astype(jnp.float32)
        ).astype(jnp.bfloat16)
        copy = pltpu.make_async_copy(held.at[part], stored.at[part], sems.at[i])
        copy.start()
        copies.append(copy)
    for copy in copies:
        copy.wait()


def new_moment(grad, moment):
    return pl.pallas_call(
        moment_kernel,
        in_specs=[INSIDE, INSIDE],
        out_specs=[INSIDE, ANYWHERE],
        out_shape=[
            pltpu.VMEM(grad.shape, grad.dtype),
            jax.ShapeDtypeStruct(grad.shape, grad.dtype),
        ],
        scratch_shapes=[pltpu.SemaphoreType.DMA((len(cuts(grad.shape[0], 960)),))],
        compiler_params=PARAMS,
        name="moment",
    )(inside(grad), inside(moment))


def transpose_kernel(*refs):
    count = len(refs) // 2
    for value, out in zip(refs[:count], refs[count:]):
        out[...] = value[...].T


def transposed(*values):
    return pl.pallas_call(
        transpose_kernel,
        in_specs=[INSIDE] * len(values),
        out_specs=[INSIDE] * len(values),
        out_shape=[pltpu.VMEM(value.shape[::-1], value.dtype) for value in values],
        compiler_params=PARAMS,
        name="transpose",
    )(*map(inside, values))


def power_kernel(*refs):
    *pieces, grad, other, grad_rows, other_rows, basis, rot, kept, sent = refs
    basis[...] = jnp.concatenate([piece[...] for piece in pieces], 0)
    rot_own = dot(basis[...], grad[...], ((1,), (0,)))
    rot_other = dot(basis[...], other[...], ((1,), (0,)))
    rot[...] = rot_own
    both = jnp.concatenate([rot_own, rot_other], 1).astype(jnp.bfloat16)
    half = kept.shape[0]
    for at, size in cuts(grad.shape[0], 768):
        part = pl.ds(at, size)
        rows = jnp.concatenate([grad_rows[:, part], other_rows[:, part]], 0)
        product = dot(both, rows, ((1,), (0,)))
        kept[:, part] = product[:half]
        sent[:, part] = product[half:].astype(jnp.bfloat16)


def power_products(pieces, grads):
    depth, rows = grads[0].shape
    count = sum(piece.shape[0] for piece in pieces)
    return pl.pallas_call(
        power_kernel,
        in_specs=[INSIDE] * (len(pieces) + len(grads)),
        out_specs=[INSIDE] * 4,
        out_shape=[
            pltpu.VMEM((count, depth), jnp.bfloat16),
            pltpu.VMEM((count, rows), jnp.float32),
            pltpu.VMEM((count // 2, depth), jnp.float32),
            pltpu.VMEM((count // 2, depth), jnp.bfloat16),
        ],
        compiler_params=PARAMS,
        name="power",
    )(*map(inside, (*pieces, *grads)))


def normal_kernel(kept, come, out):
    power = kept[...] + come[...].astype(jnp.float32)
    square = jnp.mean(power * power, axis=1, keepdims=True)
    out[...] = power / jnp.sqrt(square + 1e-06)


def normalised(kept, come):
    return pl.pallas_call(
        normal_kernel,
        in_specs=[INSIDE] * 2,
        out_specs=INSIDE,
        out_shape=jax.ShapeDtypeStruct(kept.shape, kept.dtype),
        compiler_params=PARAMS,
        name="normalise",
    )(inside(kept), inside(come))


def early(depth):
    return depth // 3 // 128 * 128


def scale_kernel(
    orders, own, basis, grad, moment, rot_half, second, scaled, second_next, update, *scratch
):
    rot, mom, value_in, held, sems = scratch
    me = lax.axis_index("rows")
    core, chip = me & 1, me >> 1
    bits = len(orders[0])
    parity = functools.reduce(lambda a, b: a ^ b, [(me >> b) & 1 for b in range(bits + 1)])
    count = rot_half.shape[0]
    rot[:count] = rot_half[...]
    rot[count:] = dot(basis[count:], grad[...], ((1,), (0,)))
    mom[...] = dot(basis[...], moment[...], ((1,), (0,)))

    def place(offset, order):
        return sum(((offset >> bit) & 1) << step for step, bit in enumerate(order)) * own

    for half in range(2):

        @pl.when(parity == half)
        def _():
            for offset in range(1 << bits):
                mine = pl.ds(place(offset, orders[half]), own)
                theirs = pl.ds(count + place(offset, orders[1 - half]), own)
                first = core == odd(offset)
                tile = pl.ds(pl.multiple_of((chip ^ offset) * 2 * own, 2 * own), 2 * own)

                def joined(ref):
                    a, b = ref[mine], ref[theirs]
                    return jnp.where(
                        first, jnp.concatenate([a, b], 0), jnp.concatenate([b, a], 0)
                    )

                turned = joined(rot)
                value = 0.95 * second[tile] + 0.05 * turned * turned
                value_in[tile] = value
                ratio = joined(mom) / (jnp.sqrt(value) + 1e-08)
                rot[mine] = jnp.where(first, ratio[:own], ratio[own:])
                rot[theirs] = jnp.where(first, ratio[own:], ratio[:own])

    copies = [pltpu.make_async_copy(value_in, second_next, sems.at[0])]
    copies[0].start()
    scaled[...] = rot[...].astype(jnp.bfloat16)
    part = pl.ds(0, held.shape[0])
    held[...] = dot(basis[:, part], scaled[...], ((0,), (0,))).astype(jnp.bfloat16)
    copies.append(pltpu.make_async_copy(held, update.at[part], sems.at[1]))
    copies[1].start()
    for copy in copies:
        copy.wait()


def scaled_rotation(orders, own, basis, grad, moment, rot_half, second):
    count, depth = basis.shape
    rows = grad.shape[1]
    return pl.pallas_call(
        functools.partial(scale_kernel, orders, own),
        in_specs=[INSIDE] * 5,
        out_specs=[INSIDE, ANYWHERE, ANYWHERE],
        out_shape=[
            pltpu.VMEM((count, rows), jnp.bfloat16),
            jax.ShapeDtypeStruct((count, rows), jnp.float32),
            jax.ShapeDtypeStruct((depth, rows), jnp.bfloat16),
        ],
        scratch_shapes=[
            pltpu.VMEM((count, rows), jnp.float32),
            pltpu.VMEM((count, rows), jnp.float32),
            pltpu.VMEM((count, rows), jnp.float32),
            pltpu.VMEM((early(depth), rows), jnp.bfloat16),
            pltpu.SemaphoreType.DMA((2,)),
        ],
        compiler_params=PARAMS,
        name="scale",
    )(*map(inside, (basis, grad, moment, rot_half, second)))


def update_kernel(basis, scaled, so_far, out, held, sems):
    first = early(out.shape[0])
    copies = []
    for i, (at, size) in enumerate(cuts(out.shape[0] - first, 768)):
        part = pl.ds(first + at, size)
        here = pl.ds(at, size)
        held[here] = dot(basis[:, part], scaled[...], ((0,), (0,))).astype(jnp.bfloat16)
        copy = pltpu.make_async_copy(held.at[here], out.at[part], sems.at[i])
        copy.start()
        copies.append(copy)
    for copy in copies:
        copy.wait()


def rest_of_update(basis, scaled, so_far):
    depth, rows = so_far.shape
    later = depth - early(depth)
    return pl.pallas_call(
        update_kernel,
        in_specs=[INSIDE, INSIDE, ANYWHERE],
        out_specs=ANYWHERE,
        out_shape=jax.ShapeDtypeStruct((depth, rows), jnp.bfloat16),
        input_output_aliases={2: 0},
        scratch_shapes=[
            pltpu.VMEM((later, rows), jnp.bfloat16),
            pltpu.SemaphoreType.DMA((len(cuts(later, 768)),)),
        ],
        compiler_params=PARAMS,
        name="update",
    )(inside(basis), inside(scaled), so_far)


def shards(n, grad, moment, second, basis):
    bits = n.bit_length() - 2
    own = basis.shape[0]
    far, near = (bits - 1,), tuple(reversed(range(bits - 1)))
    orders = (far + near, far + near[-1:] + near[:-1])

    def exchange(value, step):
        pairs = [(i, i ^ (2 << orders[odd(i)][step]) ^ 1) for i in range(n)]
        return lax.ppermute(value, "rows", pairs)

    def across(value):
        return lax.ppermute(value, "rows", [(i, i ^ 1) for i in range(n)])

    grad, moment, second = grad.T, moment.T, second.T

    come = exchange(basis, 0)
    grad, held = load(grad, basis)
    come, grad, held = tie(come, grad, held)
    other = across(grad)
    held = jnp.concatenate([held, come], 0)
    for step in range(1, bits - 2):
        held = jnp.concatenate([held, exchange(held, step)], 0)
    first = exchange(held, bits - 2)
    second_hand = exchange(held, bits - 1)
    first, grad = tie(first, grad)
    last = exchange(first, bits - 1)
    second_hand, grad, other = tie(second_hand, grad, other)
    grad_rows, other_rows = transposed(grad, other)
    last, grad_rows, other_rows = tie(last, grad_rows, other_rows)
    held, rot_half, kept, sent = power_products(
        (held, first, second_hand, last), (grad, other, grad_rows, other_rows)
    )
    come = exchange(sent, bits - 1)
    moment, _ = tie(moment, sent)
    moment_in, moment_next = new_moment(grad, moment)
    held, _ = tie(held, moment_in)
    theirs = across(held)
    come, moment_in, moment_next = tie(come, moment_in, moment_next)
    for step in reversed(range(bits)):
        if step == 0:
            break
        kept = kept + come.astype(jnp.float32)
        half = kept.shape[0] // 2
        come = exchange(kept[half:].astype(jnp.bfloat16), step - 1)
        kept = kept[:half]
        if step == bits - 1:
            theirs, kept = tie(theirs, kept)
            whole = jnp.concatenate([held, theirs], 0)
            scaled, second_next, update = scaled_rotation(
                orders, own, whole, grad, moment_in, rot_half, second
            )
            come, scaled, second_next, update = tie(come, scaled, second_next, update)
        if step == bits - 2:
            scaled, kept = tie(scaled, kept)
            update = rest_of_update(whole, scaled, update)
            come, update = tie(come, update)
    basis_next = normalised(kept, come)
    return update.T, moment_next.T, second_next.T, basis_next


def solution(mesh):
    n = mesh.shape["rows"]
    placed = P(("groups", "rows"), None)
    return jax.shard_map(
        lambda *arrays: shards(n, *arrays),
        mesh=mesh,
        in_specs=(placed,) * 4,
        out_specs=(placed,) * 4,
        check_vma=False,
    )
```

```python
import functools

import jax
import jax.numpy as jnp
from jax import lax
from jax.experimental import pallas as pl
from jax.experimental.pallas import tpu as pltpu
from jax.sharding import PartitionSpec as P

INSIDE = pl.BlockSpec(memory_space=pltpu.VMEM)
ANYWHERE = pl.BlockSpec(memory_space=pl.ANY)
PARAMS = pltpu.CompilerParams(vmem_limit_bytes=24 << 20)


def inside(value):
    return pltpu.with_memory_space_constraint(value, pltpu.VMEM)


def tie(*values):
    return lax.optimization_barrier(values)


def cuts(depth, size):
    return [(at, min(size, depth - at)) for at in range(0, depth, size)]


def odd(i):
    return i.bit_count() & 1


def dot(left, right, dims):
    return lax.dot_general(left, right, (dims, ((), ())), preferred_element_type=jnp.float32)


def load_kernel(*refs):
    count = len(refs) // 2
    sems = refs[-1]
    copies = [
        pltpu.make_async_copy(refs[i], refs[count + i], sems.at[i]) for i in range(count)
    ]
    for copy in copies:
        copy.start()
    for copy in copies:
        copy.wait()


def load(*values):
    out = pl.pallas_call(
        load_kernel,
        in_specs=[pl.BlockSpec(memory_space=pltpu.HBM)] * len(values),
        out_specs=[INSIDE] * len(values),
        out_shape=[pltpu.VMEM(value.shape, value.dtype) for value in values],
        scratch_shapes=[pltpu.SemaphoreType.DMA((len(values),))],
        compiler_params=PARAMS,
        name="load",
    )(*[pltpu.with_memory_space_constraint(value, pltpu.HBM) for value in values])
    return out


def moment_kernel(grad, moment, held, stored, sems):
    copies = []
    for i, (at, size) in enumerate(cuts(grad.shape[0], 960)):
        part = pl.ds(at, size)
        held[part] = (
            0.9 * moment[part].astype(jnp.float32) + 0.1 * grad[part].astype(jnp.float32)
        ).astype(jnp.bfloat16)
        copy = pltpu.make_async_copy(held.at[part], stored.at[part], sems.at[i])
        copy.start()
        copies.append(copy)
    for copy in copies:
        copy.wait()


def new_moment(grad, moment):
    return pl.pallas_call(
        moment_kernel,
        in_specs=[INSIDE, INSIDE],
        out_specs=[INSIDE, ANYWHERE],
        out_shape=[
            pltpu.VMEM(grad.shape, grad.dtype),
            jax.ShapeDtypeStruct(grad.shape, grad.dtype),
        ],
        scratch_shapes=[pltpu.SemaphoreType.DMA((len(cuts(grad.shape[0], 960)),))],
        compiler_params=PARAMS,
        name="moment",
    )(inside(grad), inside(moment))


def transpose_kernel(*refs):
    count = len(refs) // 2
    for value, out in zip(refs[:count], refs[count:]):
        out[...] = value[...].T


def transposed(*values):
    return pl.pallas_call(
        transpose_kernel,
        in_specs=[INSIDE] * len(values),
        out_specs=[INSIDE] * len(values),
        out_shape=[pltpu.VMEM(value.shape[::-1], value.dtype) for value in values],
        compiler_params=PARAMS,
        name="transpose",
    )(*map(inside, values))


def power_kernel(*refs):
    *pieces, grad, other, grad_rows, other_rows, basis, rot, kept, sent = refs
    basis[...] = jnp.concatenate([piece[...] for piece in pieces], 0)
    rot_own = dot(basis[...], grad[...], ((1,), (0,)))
    rot_other = dot(basis[...], other[...], ((1,), (0,)))
    rot[...] = rot_own
    both = jnp.concatenate([rot_own, rot_other], 1).astype(jnp.bfloat16)
    half = kept.shape[0]
    for at, size in cuts(grad.shape[0], 768):
        part = pl.ds(at, size)
        rows = jnp.concatenate([grad_rows[:, part], other_rows[:, part]], 0)
        product = dot(both, rows, ((1,), (0,)))
        kept[:, part] = product[:half]
        sent[:, part] = product[half:].astype(jnp.bfloat16)


def power_products(pieces, grads):
    depth, rows = grads[0].shape
    count = sum(piece.shape[0] for piece in pieces)
    return pl.pallas_call(
        power_kernel,
        in_specs=[INSIDE] * (len(pieces) + len(grads)),
        out_specs=[INSIDE] * 4,
        out_shape=[
            pltpu.VMEM((count, depth), jnp.bfloat16),
            pltpu.VMEM((count, rows), jnp.float32),
            pltpu.VMEM((count // 2, depth), jnp.float32),
            pltpu.VMEM((count // 2, depth), jnp.bfloat16),
        ],
        compiler_params=PARAMS,
        name="power",
    )(*map(inside, (*pieces, *grads)))


def normal_kernel(kept, come, out):
    power = kept[...] + come[...].astype(jnp.float32)
    square = jnp.mean(power * power, axis=1, keepdims=True)
    out[...] = power / jnp.sqrt(square + 1e-06)


def normalised(kept, come):
    return pl.pallas_call(
        normal_kernel,
        in_specs=[INSIDE] * 2,
        out_specs=INSIDE,
        out_shape=jax.ShapeDtypeStruct(kept.shape, kept.dtype),
        compiler_params=PARAMS,
        name="normalise",
    )(inside(kept), inside(come))


def scale_kernel(orders, own, basis, grad, moment, rot_half, second, scaled, second_next, rot, mom):
    me = lax.axis_index("rows")
    core, chip = me & 1, me >> 1
    bits = len(orders[0])
    parity = functools.reduce(lambda a, b: a ^ b, [(me >> b) & 1 for b in range(bits + 1)])
    count = rot_half.shape[0]
    rot[:count] = rot_half[...]
    rot[count:] = dot(basis[count:], grad[...], ((1,), (0,)))
    mom[...] = dot(basis[...], moment[...], ((1,), (0,)))

    def place(offset, order):
        return sum(((offset >> bit) & 1) << step for step, bit in enumerate(order)) * own

    for half in range(2):

        @pl.when(parity == half)
        def _():
            for offset in range(1 << bits):
                mine = pl.ds(place(offset, orders[half]), own)
                theirs = pl.ds(count + place(offset, orders[1 - half]), own)
                first = core == odd(offset)
                tile = pl.ds(pl.multiple_of((chip ^ offset) * 2 * own, 2 * own), 2 * own)

                def joined(ref):
                    a, b = ref[mine], ref[theirs]
                    return jnp.where(
                        first, jnp.concatenate([a, b], 0), jnp.concatenate([b, a], 0)
                    )

                turned = joined(rot)
                value = 0.95 * second[tile] + 0.05 * turned * turned
                second_next[tile] = value
                ratio = joined(mom) / (jnp.sqrt(value) + 1e-08)
                rot[mine] = jnp.where(first, ratio[:own], ratio[own:])
                rot[theirs] = jnp.where(first, ratio[own:], ratio[:own])

    scaled[...] = rot[...].astype(jnp.bfloat16)


def scaled_rotation(orders, own, basis, grad, moment, rot_half, second):
    count, rows = basis.shape[0], grad.shape[1]
    return pl.pallas_call(
        functools.partial(scale_kernel, orders, own),
        in_specs=[INSIDE] * 5,
        out_specs=[INSIDE] * 2,
        out_shape=[
            pltpu.VMEM((count, rows), jnp.bfloat16),
            jax.ShapeDtypeStruct((count, rows), jnp.float32),
        ],
        scratch_shapes=[pltpu.VMEM((count, rows), jnp.float32)] * 2,
        compiler_params=PARAMS,
        name="scale",
    )(*map(inside, (basis, grad, moment, rot_half, second)))


def update_kernel(basis, scaled, out, held, sems):
    copies = []
    for i, (at, size) in enumerate(cuts(out.shape[0], 640)):
        part = pl.ds(at, size)
        held[part] = dot(basis[:, part], scaled[...], ((0,), (0,))).astype(jnp.bfloat16)
        copy = pltpu.make_async_copy(held.at[part], out.at[part], sems.at[i])
        copy.start()
        copies.append(copy)
    for copy in copies:
        copy.wait()


def new_update(basis, scaled):
    depth, rows = basis.shape[1], scaled.shape[1]
    return pl.pallas_call(
        update_kernel,
        in_specs=[INSIDE] * 2,
        out_specs=ANYWHERE,
        out_shape=jax.ShapeDtypeStruct((depth, rows), jnp.bfloat16),
        scratch_shapes=[
            pltpu.VMEM((depth, rows), jnp.bfloat16),
            pltpu.SemaphoreType.DMA((len(cuts(depth, 640)),)),
        ],
        compiler_params=PARAMS,
        name="update",
    )(inside(basis), inside(scaled))


def shards(n, grad, moment, second, basis):
    bits = n.bit_length() - 2
    own = basis.shape[0]
    far, near = (bits - 1,), tuple(reversed(range(bits - 1)))
    orders = (far + near, far + near[-1:] + near[:-1])

    def exchange(value, step):
        pairs = [(i, i ^ (2 << orders[odd(i)][step]) ^ 1) for i in range(n)]
        return lax.ppermute(value, "rows", pairs)

    def across(value):
        return lax.ppermute(value, "rows", [(i, i ^ 1) for i in range(n)])

    grad, moment, second = grad.T, moment.T, second.T

    come = exchange(basis, 0)
    grad, held = load(grad, basis)
    come, grad, held = tie(come, grad, held)
    other = across(grad)
    held = jnp.concatenate([held, come], 0)
    for step in range(1, bits - 2):
        held = jnp.concatenate([held, exchange(held, step)], 0)
    first = exchange(held, bits - 2)
    second_hand = exchange(held, bits - 1)
    first, grad = tie(first, grad)
    last = exchange(first, bits - 1)
    second_hand, grad, other = tie(second_hand, grad, other)
    grad_rows, other_rows = transposed(grad, other)
    last, grad_rows, other_rows = tie(last, grad_rows, other_rows)
    held, rot_half, kept, sent = power_products(
        (held, first, second_hand, last), (grad, other, grad_rows, other_rows)
    )
    come = exchange(sent, bits - 1)
    moment, _ = tie(moment, sent)
    theirs = across(held)
    moment_in, moment_next = new_moment(grad, moment)
    come, moment_in, moment_next = tie(come, moment_in, moment_next)
    for step in reversed(range(bits)):
        if step == 0:
            break
        kept = kept + come.astype(jnp.float32)
        half = kept.shape[0] // 2
        come = exchange(kept[half:].astype(jnp.bfloat16), step - 1)
        kept = kept[:half]
        if step == bits - 1:
            theirs, kept = tie(theirs, kept)
            whole = jnp.concatenate([held, theirs], 0)
            scaled, second_next = scaled_rotation(
                orders, own, whole, grad, moment_in, rot_half, second
            )
            come, scaled, second_next = tie(come, scaled, second_next)
        if step == bits - 2:
            scaled, kept = tie(scaled, kept)
            update = new_update(whole, scaled)
            come, update = tie(come, update)
    basis_next = normalised(kept, come)
    return update.T, moment_next.T, second_next.T, basis_next


def solution(mesh):
    n = mesh.shape["rows"]
    placed = P(("groups", "rows"), None)
    return jax.shard_map(
        lambda *arrays: shards(n, *arrays),
        mesh=mesh,
        in_specs=(placed,) * 4,
        out_specs=(placed,) * 4,
        check_vma=False,
    )
```

```python
import functools

import jax
import jax.numpy as jnp
from jax import lax
from jax.experimental import pallas as pl
from jax.experimental.pallas import tpu as pltpu
from jax.sharding import PartitionSpec as P

INSIDE = pl.BlockSpec(memory_space=pltpu.VMEM)
ANYWHERE = pl.BlockSpec(memory_space=pl.ANY)
PARAMS = pltpu.CompilerParams(vmem_limit_bytes=24 << 20)


def inside(value):
    return pltpu.with_memory_space_constraint(value, pltpu.VMEM)


def tie(*values):
    return lax.optimization_barrier(values)


def cuts(depth, size):
    return [(at, min(size, depth - at)) for at in range(0, depth, size)]


def odd(i):
    return i.bit_count() & 1


def dot(left, right, dims):
    return lax.dot_general(left, right, (dims, ((), ())), preferred_element_type=jnp.float32)


def load_kernel(*refs):
    count = len(refs) // 2
    sems = refs[-1]
    copies = [
        pltpu.make_async_copy(refs[i], refs[count + i], sems.at[i]) for i in range(count)
    ]
    for copy in copies:
        copy.start()
    for copy in copies:
        copy.wait()


def load(*values):
    out = pl.pallas_call(
        load_kernel,
        in_specs=[pl.BlockSpec(memory_space=pltpu.HBM)] * len(values),
        out_specs=[INSIDE] * len(values),
        out_shape=[pltpu.VMEM(value.shape, value.dtype) for value in values],
        scratch_shapes=[pltpu.SemaphoreType.DMA((len(values),))],
        compiler_params=PARAMS,
        name="load",
    )(*[pltpu.with_memory_space_constraint(value, pltpu.HBM) for value in values])
    return out


def moment_kernel(grad, moment, held, stored, sems):
    copies = []
    for i, (at, size) in enumerate(cuts(grad.shape[0], 960)):
        part = pl.ds(at, size)
        held[part] = (
            0.9 * moment[part].astype(jnp.float32) + 0.1 * grad[part].astype(jnp.float32)
        ).astype(jnp.bfloat16)
        copy = pltpu.make_async_copy(held.at[part], stored.at[part], sems.at[i])
        copy.start()
        copies.append(copy)
    for copy in copies:
        copy.wait()


def new_moment(grad, moment):
    return pl.pallas_call(
        moment_kernel,
        in_specs=[INSIDE, INSIDE],
        out_specs=[INSIDE, ANYWHERE],
        out_shape=[
            pltpu.VMEM(grad.shape, grad.dtype),
            jax.ShapeDtypeStruct(grad.shape, grad.dtype),
        ],
        scratch_shapes=[pltpu.SemaphoreType.DMA((len(cuts(grad.shape[0], 960)),))],
        compiler_params=PARAMS,
        name="moment",
    )(inside(grad), inside(moment))


def transpose_kernel(*refs):
    count = len(refs) // 2
    for value, out in zip(refs[:count], refs[count:]):
        out[...] = value[...].T


def transposed(*values):
    return pl.pallas_call(
        transpose_kernel,
        in_specs=[INSIDE] * len(values),
        out_specs=[INSIDE] * len(values),
        out_shape=[pltpu.VMEM(value.shape[::-1], value.dtype) for value in values],
        compiler_params=PARAMS,
        name="transpose",
    )(*map(inside, values))


def power_kernel(*refs):
    *pieces, grad, other, grad_rows, other_rows, basis, rot, kept, sent = refs
    basis[...] = jnp.concatenate([piece[...] for piece in pieces], 0)
    rot_own = dot(basis[...], grad[...], ((1,), (0,)))
    rot_other = dot(basis[...], other[...], ((1,), (0,)))
    rot[...] = rot_own
    both = jnp.concatenate([rot_own, rot_other], 1).astype(jnp.bfloat16)
    half = kept.shape[0]
    for at, size in cuts(grad.shape[0], 768):
        part = pl.ds(at, size)
        rows = jnp.concatenate([grad_rows[:, part], other_rows[:, part]], 0)
        product = dot(both, rows, ((1,), (0,)))
        kept[:, part] = product[:half]
        sent[:, part] = product[half:].astype(jnp.bfloat16)


def power_products(pieces, grads):
    depth, rows = grads[0].shape
    count = sum(piece.shape[0] for piece in pieces)
    return pl.pallas_call(
        power_kernel,
        in_specs=[INSIDE] * (len(pieces) + len(grads)),
        out_specs=[INSIDE] * 4,
        out_shape=[
            pltpu.VMEM((count, depth), jnp.bfloat16),
            pltpu.VMEM((count, rows), jnp.float32),
            pltpu.VMEM((count // 2, depth), jnp.float32),
            pltpu.VMEM((count // 2, depth), jnp.bfloat16),
        ],
        compiler_params=PARAMS,
        name="power",
    )(*map(inside, (*pieces, *grads)))


def normal_kernel(kept, come, out):
    power = kept[...] + come[...].astype(jnp.float32)
    square = jnp.mean(power * power, axis=1, keepdims=True)
    out[...] = power / jnp.sqrt(square + 1e-06)


def normalised(kept, come):
    return pl.pallas_call(
        normal_kernel,
        in_specs=[INSIDE] * 2,
        out_specs=INSIDE,
        out_shape=jax.ShapeDtypeStruct(kept.shape, kept.dtype),
        compiler_params=PARAMS,
        name="normalise",
    )(inside(kept), inside(come))


def scale_kernel(orders, own, basis, grad, moment, rot_half, second, scaled, second_next, rot, mom):
    me = lax.axis_index("rows")
    core, chip = me & 1, me >> 1
    bits = len(orders[0])
    parity = functools.reduce(lambda a, b: a ^ b, [(me >> b) & 1 for b in range(bits)])
    count = rot_half.shape[0]
    rot[:count] = rot_half[...]
    rot[count:] = dot(basis[count:], grad[...], ((1,), (0,)))
    mom[...] = dot(basis[...], moment[...], ((1,), (0,)))

    def place(offset, order):
        return sum(((offset >> bit) & 1) << step for step, bit in enumerate(order)) * own

    for half in range(2):

        @pl.when(parity == half)
        def _():
            for offset in range(1 << bits):
                mine = pl.ds(place(offset, orders[half]), own)
                theirs = pl.ds(count + place(offset, orders[1 - half]), own)
                first = core == odd(offset & ((1 << (bits - 1)) - 1))
                tile = pl.ds(pl.multiple_of((chip ^ offset) * 2 * own, 2 * own), 2 * own)

                def joined(ref):
                    a, b = ref[mine], ref[theirs]
                    return jnp.where(
                        first, jnp.concatenate([a, b], 0), jnp.concatenate([b, a], 0)
                    )

                turned = joined(rot)
                value = 0.95 * second[tile] + 0.05 * turned * turned
                second_next[tile] = value
                ratio = joined(mom) / (jnp.sqrt(value) + 1e-08)
                rot[mine] = jnp.where(first, ratio[:own], ratio[own:])
                rot[theirs] = jnp.where(first, ratio[own:], ratio[:own])

    scaled[...] = rot[...].astype(jnp.bfloat16)


def scaled_rotation(orders, own, basis, grad, moment, rot_half, second):
    count, rows = basis.shape[0], grad.shape[1]
    return pl.pallas_call(
        functools.partial(scale_kernel, orders, own),
        in_specs=[INSIDE] * 5,
        out_specs=[INSIDE] * 2,
        out_shape=[
            pltpu.VMEM((count, rows), jnp.bfloat16),
            jax.ShapeDtypeStruct((count, rows), jnp.float32),
        ],
        scratch_shapes=[pltpu.VMEM((count, rows), jnp.float32)] * 2,
        compiler_params=PARAMS,
        name="scale",
    )(*map(inside, (basis, grad, moment, rot_half, second)))


def update_kernel(basis, scaled, out, held, sems):
    copies = []
    for i, (at, size) in enumerate(cuts(out.shape[0], 640)):
        part = pl.ds(at, size)
        held[part] = dot(basis[:, part], scaled[...], ((0,), (0,))).astype(jnp.bfloat16)
        copy = pltpu.make_async_copy(held.at[part], out.at[part], sems.at[i])
        copy.start()
        copies.append(copy)
    for copy in copies:
        copy.wait()


def new_update(basis, scaled):
    depth, rows = basis.shape[1], scaled.shape[1]
    return pl.pallas_call(
        update_kernel,
        in_specs=[INSIDE] * 2,
        out_specs=ANYWHERE,
        out_shape=jax.ShapeDtypeStruct((depth, rows), jnp.bfloat16),
        scratch_shapes=[
            pltpu.VMEM((depth, rows), jnp.bfloat16),
            pltpu.SemaphoreType.DMA((len(cuts(depth, 640)),)),
        ],
        compiler_params=PARAMS,
        name="update",
    )(inside(basis), inside(scaled))


def shards(n, grad, moment, second, basis):
    bits = n.bit_length() - 2
    own = basis.shape[0]
    far, near = (bits - 1,), tuple(reversed(range(bits - 1)))
    orders = (far + near, far + near[-1:] + near[:-1])

    def partner(i, step):
        bit = orders[odd(i & (n // 2 - 1))][step]
        return i ^ (2 << bit) ^ (bit != far[0])

    def exchange(value, step):
        return lax.ppermute(value, "rows", [(i, partner(i, step)) for i in range(n)])

    def across(value):
        return lax.ppermute(value, "rows", [(i, i ^ 1) for i in range(n)])

    grad, moment, second = grad.T, moment.T, second.T

    come = exchange(basis, 0)
    grad, held = load(grad, basis)
    come, grad, held = tie(come, grad, held)
    other = across(grad)
    held = jnp.concatenate([held, come], 0)
    for step in range(1, bits - 2):
        held = jnp.concatenate([held, exchange(held, step)], 0)
    first = exchange(held, bits - 2)
    second_hand = exchange(held, bits - 1)
    first, grad = tie(first, grad)
    last = exchange(first, bits - 1)
    second_hand, grad, other = tie(second_hand, grad, other)
    grad_rows, other_rows = transposed(grad, other)
    last, grad_rows, other_rows = tie(last, grad_rows, other_rows)
    held, rot_half, kept, sent = power_products(
        (held, first, second_hand, last), (grad, other, grad_rows, other_rows)
    )
    come = exchange(sent, bits - 1)
    moment, _ = tie(moment, sent)
    theirs = across(held)
    moment_in, moment_next = new_moment(grad, moment)
    come, moment_in, moment_next = tie(come, moment_in, moment_next)
    for step in reversed(range(bits)):
        if step == 0:
            break
        kept = kept + come.astype(jnp.float32)
        half = kept.shape[0] // 2
        come = exchange(kept[half:].astype(jnp.bfloat16), step - 1)
        kept = kept[:half]
        if step == bits - 1:
            theirs, kept = tie(theirs, kept)
            whole = jnp.concatenate([held, theirs], 0)
            scaled, second_next = scaled_rotation(
                orders, own, whole, grad, moment_in, rot_half, second
            )
            come, scaled, second_next = tie(come, scaled, second_next)
        if step == bits - 2:
            scaled, kept = tie(scaled, kept)
            update = new_update(whole, scaled)
            come, update = tie(come, update)
    basis_next = normalised(kept, come)
    return update.T, moment_next.T, second_next.T, basis_next


def solution(mesh):
    n = mesh.shape["rows"]
    placed = P(("groups", "rows"), None)
    return jax.shard_map(
        lambda *arrays: shards(n, *arrays),
        mesh=mesh,
        in_specs=(placed,) * 4,
        out_specs=(placed,) * 4,
        check_vma=False,
    )
```

```python
import functools

import jax
import jax.numpy as jnp
from jax import lax
from jax.experimental import pallas as pl
from jax.experimental.pallas import tpu as pltpu
from jax.sharding import PartitionSpec as P

INSIDE = pl.BlockSpec(memory_space=pltpu.VMEM)
ANYWHERE = pl.BlockSpec(memory_space=pl.ANY)
PARAMS = pltpu.CompilerParams(vmem_limit_bytes=24 << 20)


def inside(value):
    return pltpu.with_memory_space_constraint(value, pltpu.VMEM)


def tie(*values):
    return lax.optimization_barrier(values)


def cuts(depth, size):
    return [(at, min(size, depth - at)) for at in range(0, depth, size)]


def odd(i):
    return i.bit_count() & 1


def dot(left, right, dims):
    return lax.dot_general(left, right, (dims, ((), ())), preferred_element_type=jnp.float32)


def load_kernel(*refs):
    count = len(refs) // 2
    sems = refs[-1]
    copies = [
        pltpu.make_async_copy(refs[i], refs[count + i], sems.at[i]) for i in range(count)
    ]
    for copy in copies:
        copy.start()
    for copy in copies:
        copy.wait()


def load(*values):
    out = pl.pallas_call(
        load_kernel,
        in_specs=[pl.BlockSpec(memory_space=pltpu.HBM)] * len(values),
        out_specs=[INSIDE] * len(values),
        out_shape=[pltpu.VMEM(value.shape, value.dtype) for value in values],
        scratch_shapes=[pltpu.SemaphoreType.DMA((len(values),))],
        compiler_params=PARAMS,
        name="load",
    )(*[pltpu.with_memory_space_constraint(value, pltpu.HBM) for value in values])
    return out


def moment_kernel(grad, moment, held, stored, sems):
    copies = []
    for i, (at, size) in enumerate(cuts(grad.shape[0], 960)):
        part = pl.ds(at, size)
        held[part] = (
            0.9 * moment[part].astype(jnp.float32) + 0.1 * grad[part].astype(jnp.float32)
        ).astype(jnp.bfloat16)
        copy = pltpu.make_async_copy(held.at[part], stored.at[part], sems.at[i])
        copy.start()
        copies.append(copy)
    for copy in copies:
        copy.wait()


def new_moment(grad, moment):
    return pl.pallas_call(
        moment_kernel,
        in_specs=[INSIDE, INSIDE],
        out_specs=[INSIDE, ANYWHERE],
        out_shape=[
            pltpu.VMEM(grad.shape, grad.dtype),
            jax.ShapeDtypeStruct(grad.shape, grad.dtype),
        ],
        scratch_shapes=[pltpu.SemaphoreType.DMA((len(cuts(grad.shape[0], 960)),))],
        compiler_params=PARAMS,
        name="moment",
    )(inside(grad), inside(moment))


def transpose_kernel(*refs):
    count = len(refs) // 2
    for value, out in zip(refs[:count], refs[count:]):
        out[...] = value[...].T


def transposed(*values):
    return pl.pallas_call(
        transpose_kernel,
        in_specs=[INSIDE] * len(values),
        out_specs=[INSIDE] * len(values),
        out_shape=[pltpu.VMEM(value.shape[::-1], value.dtype) for value in values],
        compiler_params=PARAMS,
        name="transpose",
    )(*map(inside, values))


def power_kernel(*refs):
    *pieces, grad, other, grad_rows, other_rows, basis, rot, kept, sent = refs
    basis[...] = jnp.concatenate([piece[...] for piece in pieces], 0)
    rot_own = dot(basis[...], grad[...], ((1,), (0,)))
    rot_other = dot(basis[...], other[...], ((1,), (0,)))
    rot[...] = rot_own
    both = jnp.concatenate([rot_own, rot_other], 1).astype(jnp.bfloat16)
    half = kept.shape[0]
    for at, size in cuts(grad.shape[0], 768):
        part = pl.ds(at, size)
        rows = jnp.concatenate([grad_rows[:, part], other_rows[:, part]], 0)
        product = dot(both, rows, ((1,), (0,)))
        kept[:, part] = product[:half]
        sent[:, part] = product[half:].astype(jnp.bfloat16)


def power_products(pieces, grads):
    depth, rows = grads[0].shape
    count = sum(piece.shape[0] for piece in pieces)
    return pl.pallas_call(
        power_kernel,
        in_specs=[INSIDE] * (len(pieces) + len(grads)),
        out_specs=[INSIDE] * 4,
        out_shape=[
            pltpu.VMEM((count, depth), jnp.bfloat16),
            pltpu.VMEM((count, rows), jnp.float32),
            pltpu.VMEM((count // 2, depth), jnp.float32),
            pltpu.VMEM((count // 2, depth), jnp.bfloat16),
        ],
        compiler_params=PARAMS,
        name="power",
    )(*map(inside, (*pieces, *grads)))


def normal_kernel(kept, come, out):
    power = kept[...] + come[...].astype(jnp.float32)
    square = jnp.mean(power * power, axis=1, keepdims=True)
    out[...] = power / jnp.sqrt(square + 1e-06)


def normalised(kept, come):
    return pl.pallas_call(
        normal_kernel,
        in_specs=[INSIDE] * 2,
        out_specs=INSIDE,
        out_shape=jax.ShapeDtypeStruct(kept.shape, kept.dtype),
        compiler_params=PARAMS,
        name="normalise",
    )(inside(kept), inside(come))


def early(depth):
    return min(256, depth)


def scale_kernel(
    orders, own, basis, grad, moment, rot_half, second, scaled, second_next, update, *scratch
):
    rot, mom, value_in, held, sems = scratch
    me = lax.axis_index("rows")
    core, chip = me & 1, me >> 1
    bits = len(orders[0])
    parity = functools.reduce(lambda a, b: a ^ b, [(me >> b) & 1 for b in range(bits + 1)])
    count = rot_half.shape[0]
    rot[:count] = rot_half[...]
    rot[count:] = dot(basis[count:], grad[...], ((1,), (0,)))
    mom[...] = dot(basis[...], moment[...], ((1,), (0,)))

    def place(offset, order):
        return sum(((offset >> bit) & 1) << step for step, bit in enumerate(order)) * own

    for half in range(2):

        @pl.when(parity == half)
        def _():
            for offset in range(1 << bits):
                mine = pl.ds(place(offset, orders[half]), own)
                theirs = pl.ds(count + place(offset, orders[1 - half]), own)
                first = core == odd(offset)
                tile = pl.ds(pl.multiple_of((chip ^ offset) * 2 * own, 2 * own), 2 * own)

                def joined(ref):
                    a, b = ref[mine], ref[theirs]
                    return jnp.where(
                        first, jnp.concatenate([a, b], 0), jnp.concatenate([b, a], 0)
                    )

                turned = joined(rot)
                value = 0.95 * second[tile] + 0.05 * turned * turned
                value_in[tile] = value
                ratio = joined(mom) / (jnp.sqrt(value) + 1e-08)
                rot[mine] = jnp.where(first, ratio[:own], ratio[own:])
                rot[theirs] = jnp.where(first, ratio[own:], ratio[:own])

    copies = [pltpu.make_async_copy(value_in, second_next, sems.at[0])]
    copies[0].start()
    scaled[...] = rot[...].astype(jnp.bfloat16)
    part = pl.ds(0, held.shape[0])
    held[...] = dot(basis[:, part], scaled[...], ((0,), (0,))).astype(jnp.bfloat16)
    copies.append(pltpu.make_async_copy(held, update.at[part], sems.at[1]))
    copies[1].start()
    for copy in copies:
        copy.wait()


def scaled_rotation(orders, own, basis, grad, moment, rot_half, second):
    count, depth = basis.shape
    rows = grad.shape[1]
    return pl.pallas_call(
        functools.partial(scale_kernel, orders, own),
        in_specs=[INSIDE] * 5,
        out_specs=[INSIDE, ANYWHERE, ANYWHERE],
        out_shape=[
            pltpu.VMEM((count, rows), jnp.bfloat16),
            jax.ShapeDtypeStruct((count, rows), jnp.float32),
            jax.ShapeDtypeStruct((depth, rows), jnp.bfloat16),
        ],
        scratch_shapes=[
            pltpu.VMEM((count, rows), jnp.float32),
            pltpu.VMEM((count, rows), jnp.float32),
            pltpu.VMEM((count, rows), jnp.float32),
            pltpu.VMEM((early(depth), rows), jnp.bfloat16),
            pltpu.SemaphoreType.DMA((2,)),
        ],
        compiler_params=PARAMS,
        name="scale",
    )(*map(inside, (basis, grad, moment, rot_half, second)))


def update_kernel(basis, scaled, so_far, out, held, sems):
    first = early(out.shape[0])
    copies = []
    for i, (at, size) in enumerate(cuts(out.shape[0] - first, 384)):
        part = pl.ds(first + at, size)
        here = pl.ds(at, size)
        held[here] = dot(basis[:, part], scaled[...], ((0,), (0,))).astype(jnp.bfloat16)
        copy = pltpu.make_async_copy(held.at[here], out.at[part], sems.at[i])
        copy.start()
        copies.append(copy)
    for copy in copies:
        copy.wait()


def rest_of_update(basis, scaled, so_far):
    depth, rows = so_far.shape
    later = depth - early(depth)
    return pl.pallas_call(
        update_kernel,
        in_specs=[INSIDE, INSIDE, ANYWHERE],
        out_specs=ANYWHERE,
        out_shape=jax.ShapeDtypeStruct((depth, rows), jnp.bfloat16),
        input_output_aliases={2: 0},
        scratch_shapes=[
            pltpu.VMEM((later, rows), jnp.bfloat16),
            pltpu.SemaphoreType.DMA((len(cuts(later, 384)),)),
        ],
        compiler_params=PARAMS,
        name="update",
    )(inside(basis), inside(scaled), so_far)


def shards(n, grad, moment, second, basis):
    bits = n.bit_length() - 2
    own = basis.shape[0]
    far, near = (bits - 1,), tuple(reversed(range(bits - 1)))
    orders = (far + near, far + near[-1:] + near[:-1])

    def exchange(value, step):
        pairs = [(i, i ^ (2 << orders[odd(i)][step]) ^ 1) for i in range(n)]
        return lax.ppermute(value, "rows", pairs)

    def across(value):
        return lax.ppermute(value, "rows", [(i, i ^ 1) for i in range(n)])

    grad, moment, second = grad.T, moment.T, second.T

    come = exchange(basis, 0)
    grad, held = load(grad, basis)
    come, grad, held = tie(come, grad, held)
    other = across(grad)
    held = jnp.concatenate([held, come], 0)
    for step in range(1, bits - 2):
        held = jnp.concatenate([held, exchange(held, step)], 0)
    first = exchange(held, bits - 2)
    second_hand = exchange(held, bits - 1)
    first, grad = tie(first, grad)
    last = exchange(first, bits - 1)
    second_hand, grad, other = tie(second_hand, grad, other)
    grad_rows, other_rows = transposed(grad, other)
    last, grad_rows, other_rows = tie(last, grad_rows, other_rows)
    held, rot_half, kept, sent = power_products(
        (held, first, second_hand, last), (grad, other, grad_rows, other_rows)
    )
    come = exchange(sent, bits - 1)
    moment, _ = tie(moment, sent)
    theirs = across(held)
    moment_in, moment_next = new_moment(grad, moment)
    come, moment_in, moment_next = tie(come, moment_in, moment_next)
    for step in reversed(range(bits)):
        if step == 0:
            break
        kept = kept + come.astype(jnp.float32)
        half = kept.shape[0] // 2
        come = exchange(kept[half:].astype(jnp.bfloat16), step - 1)
        kept = kept[:half]
        if step == bits - 1:
            theirs, kept = tie(theirs, kept)
            whole = jnp.concatenate([held, theirs], 0)
            scaled, second_next, update = scaled_rotation(
                orders, own, whole, grad, moment_in, rot_half, second
            )
            come, scaled, second_next, update = tie(come, scaled, second_next, update)
        if step == bits - 2:
            scaled, kept = tie(scaled, kept)
            update = rest_of_update(whole, scaled, update)
            come, update = tie(come, update)
    basis_next = normalised(kept, come)
    return update.T, moment_next.T, second_next.T, basis_next


def solution(mesh):
    n = mesh.shape["rows"]
    placed = P(("groups", "rows"), None)
    return jax.shard_map(
        lambda *arrays: shards(n, *arrays),
        mesh=mesh,
        in_specs=(placed,) * 4,
        out_specs=(placed,) * 4,
        check_vma=False,
    )
```

```python
import functools

import jax
import jax.numpy as jnp
from jax import lax
from jax.experimental import pallas as pl
from jax.experimental.pallas import tpu as pltpu
from jax.sharding import PartitionSpec as P

INSIDE = pl.BlockSpec(memory_space=pltpu.VMEM)
ANYWHERE = pl.BlockSpec(memory_space=pl.ANY)
PARAMS = pltpu.CompilerParams(vmem_limit_bytes=24 << 20)


def inside(value):
    return pltpu.with_memory_space_constraint(value, pltpu.VMEM)


def tie(*values):
    return lax.optimization_barrier(values)


def cuts(depth, size):
    return [(at, min(size, depth - at)) for at in range(0, depth, size)]


def odd(i):
    return i.bit_count() & 1


def dot(left, right, dims):
    return lax.dot_general(left, right, (dims, ((), ())), preferred_element_type=jnp.float32)


def load_kernel(*refs):
    count = len(refs) // 2
    sems = refs[-1]
    copies = [
        pltpu.make_async_copy(refs[i], refs[count + i], sems.at[i]) for i in range(count)
    ]
    for copy in copies:
        copy.start()
    for copy in copies:
        copy.wait()


def load(*values):
    out = pl.pallas_call(
        load_kernel,
        in_specs=[pl.BlockSpec(memory_space=pltpu.HBM)] * len(values),
        out_specs=[INSIDE] * len(values),
        out_shape=[pltpu.VMEM(value.shape, value.dtype) for value in values],
        scratch_shapes=[pltpu.SemaphoreType.DMA((len(values),))],
        compiler_params=PARAMS,
        name="load",
    )(*[pltpu.with_memory_space_constraint(value, pltpu.HBM) for value in values])
    return out


def moment_kernel(grad, moment, held, stored, sems):
    copies = []
    for i, (at, size) in enumerate(cuts(grad.shape[0], 960)):
        part = pl.ds(at, size)
        held[part] = (
            0.9 * moment[part].astype(jnp.float32) + 0.1 * grad[part].astype(jnp.float32)
        ).astype(jnp.bfloat16)
        copy = pltpu.make_async_copy(held.at[part], stored.at[part], sems.at[i])
        copy.start()
        copies.append(copy)
    for copy in copies:
        copy.wait()


def new_moment(grad, moment):
    return pl.pallas_call(
        moment_kernel,
        in_specs=[INSIDE, INSIDE],
        out_specs=[INSIDE, ANYWHERE],
        out_shape=[
            pltpu.VMEM(grad.shape, grad.dtype),
            jax.ShapeDtypeStruct(grad.shape, grad.dtype),
        ],
        scratch_shapes=[pltpu.SemaphoreType.DMA((len(cuts(grad.shape[0], 960)),))],
        compiler_params=PARAMS,
        name="moment",
    )(inside(grad), inside(moment))


def transpose_kernel(*refs):
    count = len(refs) // 2
    for value, out in zip(refs[:count], refs[count:]):
        out[...] = value[...].T


def transposed(*values):
    return pl.pallas_call(
        transpose_kernel,
        in_specs=[INSIDE] * len(values),
        out_specs=[INSIDE] * len(values),
        out_shape=[pltpu.VMEM(value.shape[::-1], value.dtype) for value in values],
        compiler_params=PARAMS,
        name="transpose",
    )(*map(inside, values))


def power_kernel(*refs):
    *pieces, grad, other, grad_rows, other_rows, basis, rot, kept, sent = refs
    basis[...] = jnp.concatenate([piece[...] for piece in pieces], 0)
    rot_own = dot(basis[...], grad[...], ((1,), (0,)))
    rot_other = dot(basis[...], other[...], ((1,), (0,)))
    rot[...] = rot_own
    both = jnp.concatenate([rot_own, rot_other], 1).astype(jnp.bfloat16)
    half = kept.shape[0]
    for at, size in cuts(grad.shape[0], 768):
        part = pl.ds(at, size)
        rows = jnp.concatenate([grad_rows[:, part], other_rows[:, part]], 0)
        product = dot(both, rows, ((1,), (0,)))
        kept[:, part] = product[:half]
        sent[:, part] = product[half:].astype(jnp.bfloat16)


def power_products(pieces, grads):
    depth, rows = grads[0].shape
    count = sum(piece.shape[0] for piece in pieces)
    return pl.pallas_call(
        power_kernel,
        in_specs=[INSIDE] * (len(pieces) + len(grads)),
        out_specs=[INSIDE] * 4,
        out_shape=[
            pltpu.VMEM((count, depth), jnp.bfloat16),
            pltpu.VMEM((count, rows), jnp.float32),
            pltpu.VMEM((count // 2, depth), jnp.float32),
            pltpu.VMEM((count // 2, depth), jnp.bfloat16),
        ],
        compiler_params=PARAMS,
        name="power",
    )(*map(inside, (*pieces, *grads)))


def normal_kernel(kept, come, out):
    power = kept[...] + come[...].astype(jnp.float32)
    square = jnp.mean(power * power, axis=1, keepdims=True)
    out[...] = power / jnp.sqrt(square + 1e-06)


def normalised(kept, come):
    return pl.pallas_call(
        normal_kernel,
        in_specs=[INSIDE] * 2,
        out_specs=INSIDE,
        out_shape=jax.ShapeDtypeStruct(kept.shape, kept.dtype),
        compiler_params=PARAMS,
        name="normalise",
    )(inside(kept), inside(come))


def early(depth):
    return min(256, depth)


def scale_kernel(
    orders, own, basis, grad, moment, rot_half, second, scaled, second_next, update, *scratch
):
    rot, mom, value_in, held, sems = scratch
    me = lax.axis_index("rows")
    core, chip = me & 1, me >> 1
    bits = len(orders[0])
    parity = functools.reduce(lambda a, b: a ^ b, [(me >> b) & 1 for b in range(bits)])
    count = rot_half.shape[0]
    rot[:count] = rot_half[...]
    rot[count:] = dot(basis[count:], grad[...], ((1,), (0,)))
    mom[...] = dot(basis[...], moment[...], ((1,), (0,)))

    def place(offset, order):
        return sum(((offset >> bit) & 1) << step for step, bit in enumerate(order)) * own

    for half in range(2):

        @pl.when(parity == half)
        def _():
            for offset in range(1 << bits):
                mine = pl.ds(place(offset, orders[half]), own)
                theirs = pl.ds(count + place(offset, orders[1 - half]), own)
                first = core == odd(offset & ((1 << (bits - 1)) - 1))
                tile = pl.ds(pl.multiple_of((chip ^ offset) * 2 * own, 2 * own), 2 * own)

                def joined(ref):
                    a, b = ref[mine], ref[theirs]
                    return jnp.where(
                        first, jnp.concatenate([a, b], 0), jnp.concatenate([b, a], 0)
                    )

                turned = joined(rot)
                value = 0.95 * second[tile] + 0.05 * turned * turned
                value_in[tile] = value
                ratio = joined(mom) / (jnp.sqrt(value) + 1e-08)
                rot[mine] = jnp.where(first, ratio[:own], ratio[own:])
                rot[theirs] = jnp.where(first, ratio[own:], ratio[:own])

    copies = [pltpu.make_async_copy(value_in, second_next, sems.at[0])]
    copies[0].start()
    scaled[...] = rot[...].astype(jnp.bfloat16)
    part = pl.ds(0, held.shape[0])
    held[...] = dot(basis[:, part], scaled[...], ((0,), (0,))).astype(jnp.bfloat16)
    copies.append(pltpu.make_async_copy(held, update.at[part], sems.at[1]))
    copies[1].start()
    for copy in copies:
        copy.wait()


def scaled_rotation(orders, own, basis, grad, moment, rot_half, second):
    count, depth = basis.shape
    rows = grad.shape[1]
    return pl.pallas_call(
        functools.partial(scale_kernel, orders, own),
        in_specs=[INSIDE] * 5,
        out_specs=[INSIDE, ANYWHERE, ANYWHERE],
        out_shape=[
            pltpu.VMEM((count, rows), jnp.bfloat16),
            jax.ShapeDtypeStruct((count, rows), jnp.float32),
            jax.ShapeDtypeStruct((depth, rows), jnp.bfloat16),
        ],
        scratch_shapes=[
            pltpu.VMEM((count, rows), jnp.float32),
            pltpu.VMEM((count, rows), jnp.float32),
            pltpu.VMEM((count, rows), jnp.float32),
            pltpu.VMEM((early(depth), rows), jnp.bfloat16),
            pltpu.SemaphoreType.DMA((2,)),
        ],
        compiler_params=PARAMS,
        name="scale",
    )(*map(inside, (basis, grad, moment, rot_half, second)))


def update_kernel(basis, scaled, so_far, out, held, sems):
    first = early(out.shape[0])
    copies = []
    for i, (at, size) in enumerate(cuts(out.shape[0] - first, 384)):
        part = pl.ds(first + at, size)
        here = pl.ds(at, size)
        held[here] = dot(basis[:, part], scaled[...], ((0,), (0,))).astype(jnp.bfloat16)
        copy = pltpu.make_async_copy(held.at[here], out.at[part], sems.at[i])
        copy.start()
        copies.append(copy)
    for copy in copies:
        copy.wait()


def rest_of_update(basis, scaled, so_far):
    depth, rows = so_far.shape
    later = depth - early(depth)
    return pl.pallas_call(
        update_kernel,
        in_specs=[INSIDE, INSIDE, ANYWHERE],
        out_specs=ANYWHERE,
        out_shape=jax.ShapeDtypeStruct((depth, rows), jnp.bfloat16),
        input_output_aliases={2: 0},
        scratch_shapes=[
            pltpu.VMEM((later, rows), jnp.bfloat16),
            pltpu.SemaphoreType.DMA((len(cuts(later, 384)),)),
        ],
        compiler_params=PARAMS,
        name="update",
    )(inside(basis), inside(scaled), so_far)


def shards(n, grad, moment, second, basis):
    bits = n.bit_length() - 2
    own = basis.shape[0]
    far, near = (bits - 1,), tuple(reversed(range(bits - 1)))
    orders = (far + near, far + near[-1:] + near[:-1])

    def partner(i, step):
        bit = orders[odd(i & (n // 2 - 1))][step]
        return i ^ (2 << bit) ^ (bit != far[0])

    def exchange(value, step):
        return lax.ppermute(value, "rows", [(i, partner(i, step)) for i in range(n)])

    def across(value):
        return lax.ppermute(value, "rows", [(i, i ^ 1) for i in range(n)])

    grad, moment, second = grad.T, moment.T, second.T

    come = exchange(basis, 0)
    grad, held = load(grad, basis)
    come, grad, held = tie(come, grad, held)
    other = across(grad)
    held = jnp.concatenate([held, come], 0)
    for step in range(1, bits - 2):
        held = jnp.concatenate([held, exchange(held, step)], 0)
    first = exchange(held, bits - 2)
    second_hand = exchange(held, bits - 1)
    first, grad = tie(first, grad)
    last = exchange(first, bits - 1)
    second_hand, grad, other = tie(second_hand, grad, other)
    grad_rows, other_rows = transposed(grad, other)
    last, grad_rows, other_rows = tie(last, grad_rows, other_rows)
    held, rot_half, kept, sent = power_products(
        (held, first, second_hand, last), (grad, other, grad_rows, other_rows)
    )
    come = exchange(sent, bits - 1)
    moment, _ = tie(moment, sent)
    theirs = across(held)
    moment_in, moment_next = new_moment(grad, moment)
    come, moment_in, moment_next = tie(come, moment_in, moment_next)
    for step in reversed(range(bits)):
        if step == 0:
            break
        kept = kept + come.astype(jnp.float32)
        half = kept.shape[0] // 2
        come = exchange(kept[half:].astype(jnp.bfloat16), step - 1)
        kept = kept[:half]
        if step == bits - 1:
            theirs, kept = tie(theirs, kept)
            whole = jnp.concatenate([held, theirs], 0)
            scaled, second_next, update = scaled_rotation(
                orders, own, whole, grad, moment_in, rot_half, second
            )
            come, scaled, second_next, update = tie(come, scaled, second_next, update)
        if step == bits - 2:
            scaled, kept = tie(scaled, kept)
            update = rest_of_update(whole, scaled, update)
            come, update = tie(come, update)
    basis_next = normalised(kept, come)
    return update.T, moment_next.T, second_next.T, basis_next


def solution(mesh):
    n = mesh.shape["rows"]
    placed = P(("groups", "rows"), None)
    return jax.shard_map(
        lambda *arrays: shards(n, *arrays),
        mesh=mesh,
        in_specs=(placed,) * 4,
        out_specs=(placed,) * 4,
        check_vma=False,
    )
```

```python
import functools

import jax
import jax.numpy as jnp
from jax import lax
from jax.experimental import pallas as pl
from jax.experimental.pallas import tpu as pltpu
from jax.sharding import PartitionSpec as P

INSIDE = pl.BlockSpec(memory_space=pltpu.VMEM)
ANYWHERE = pl.BlockSpec(memory_space=pl.ANY)
PARAMS = pltpu.CompilerParams(vmem_limit_bytes=24 << 20)


def inside(value):
    return pltpu.with_memory_space_constraint(value, pltpu.VMEM)


def tie(*values):
    return lax.optimization_barrier(values)


def cuts(depth, size):
    return [(at, min(size, depth - at)) for at in range(0, depth, size)]


def odd(i):
    return i.bit_count() & 1


def dot(left, right, dims):
    return lax.dot_general(left, right, (dims, ((), ())), preferred_element_type=jnp.float32)


def load_kernel(*refs):
    count = len(refs) // 2
    sems = refs[-1]
    copies = [
        pltpu.make_async_copy(refs[i], refs[count + i], sems.at[i]) for i in range(count)
    ]
    for copy in copies:
        copy.start()
    for copy in copies:
        copy.wait()


def load(*values):
    out = pl.pallas_call(
        load_kernel,
        in_specs=[pl.BlockSpec(memory_space=pltpu.HBM)] * len(values),
        out_specs=[INSIDE] * len(values),
        out_shape=[pltpu.VMEM(value.shape, value.dtype) for value in values],
        scratch_shapes=[pltpu.SemaphoreType.DMA((len(values),))],
        compiler_params=PARAMS,
        name="load",
    )(*[pltpu.with_memory_space_constraint(value, pltpu.HBM) for value in values])
    return out


def moment_kernel(grad, moment, held, stored, sems):
    copies = []
    for i, (at, size) in enumerate(cuts(grad.shape[0], 960)):
        part = pl.ds(at, size)
        held[part] = (
            0.9 * moment[part].astype(jnp.float32) + 0.1 * grad[part].astype(jnp.float32)
        ).astype(jnp.bfloat16)
        copy = pltpu.make_async_copy(held.at[part], stored.at[part], sems.at[i])
        copy.start()
        copies.append(copy)
    for copy in copies:
        copy.wait()


def new_moment(grad, moment):
    return pl.pallas_call(
        moment_kernel,
        in_specs=[INSIDE, INSIDE],
        out_specs=[INSIDE, ANYWHERE],
        out_shape=[
            pltpu.VMEM(grad.shape, grad.dtype),
            jax.ShapeDtypeStruct(grad.shape, grad.dtype),
        ],
        scratch_shapes=[pltpu.SemaphoreType.DMA((len(cuts(grad.shape[0], 960)),))],
        compiler_params=PARAMS,
        name="moment",
    )(inside(grad), inside(moment))


def transpose_kernel(*refs):
    count = len(refs) // 2
    for value, out in zip(refs[:count], refs[count:]):
        out[...] = value[...].T


def transposed(*values):
    return pl.pallas_call(
        transpose_kernel,
        in_specs=[INSIDE] * len(values),
        out_specs=[INSIDE] * len(values),
        out_shape=[pltpu.VMEM(value.shape[::-1], value.dtype) for value in values],
        compiler_params=PARAMS,
        name="transpose",
    )(*map(inside, values))


def power_kernel(*refs):
    *pieces, grad, other, grad_rows, other_rows, basis, rot, kept, sent = refs
    basis[...] = jnp.concatenate([piece[...] for piece in pieces], 0)
    rot_own = dot(basis[...], grad[...], ((1,), (0,)))
    rot_other = dot(basis[...], other[...], ((1,), (0,)))
    rot[...] = rot_own
    both = jnp.concatenate([rot_own, rot_other], 1).astype(jnp.bfloat16)
    half = kept.shape[0]
    for at, size in cuts(grad.shape[0], 768):
        part = pl.ds(at, size)
        rows = jnp.concatenate([grad_rows[:, part], other_rows[:, part]], 0)
        product = dot(both, rows, ((1,), (0,)))
        kept[:, part] = product[:half]
        sent[:, part] = product[half:].astype(jnp.bfloat16)


def power_products(pieces, grads):
    depth, rows = grads[0].shape
    count = sum(piece.shape[0] for piece in pieces)
    return pl.pallas_call(
        power_kernel,
        in_specs=[INSIDE] * (len(pieces) + len(grads)),
        out_specs=[INSIDE] * 4,
        out_shape=[
            pltpu.VMEM((count, depth), jnp.bfloat16),
            pltpu.VMEM((count, rows), jnp.float32),
            pltpu.VMEM((count // 2, depth), jnp.float32),
            pltpu.VMEM((count // 2, depth), jnp.bfloat16),
        ],
        compiler_params=PARAMS,
        name="power",
    )(*map(inside, (*pieces, *grads)))


def normal_kernel(kept, come, out):
    power = kept[...] + come[...].astype(jnp.float32)
    square = jnp.mean(power * power, axis=1, keepdims=True)
    out[...] = power / jnp.sqrt(square + 1e-06)


def normalised(kept, come):
    return pl.pallas_call(
        normal_kernel,
        in_specs=[INSIDE] * 2,
        out_specs=INSIDE,
        out_shape=jax.ShapeDtypeStruct(kept.shape, kept.dtype),
        compiler_params=PARAMS,
        name="normalise",
    )(inside(kept), inside(come))


def scale_kernel(orders, own, basis, grad, moment, rot_half, second, scaled, second_next, rot, mom):
    me = lax.axis_index("rows")
    core, chip = me & 1, me >> 1
    bits = len(orders[0])
    parity = functools.reduce(lambda a, b: a ^ b, [(me >> b) & 1 for b in range(bits + 1)])
    count = rot_half.shape[0]
    rot[:count] = rot_half[...]
    rot[count:] = dot(basis[count:], grad[...], ((1,), (0,)))
    mom[...] = dot(basis[...], moment[...], ((1,), (0,)))

    def place(offset, order):
        return sum(((offset >> bit) & 1) << step for step, bit in enumerate(order)) * own

    for half in range(2):

        @pl.when(parity == half)
        def _():
            for offset in range(1 << bits):
                mine = pl.ds(place(offset, orders[half]), own)
                theirs = pl.ds(count + place(offset, orders[1 - half]), own)
                first = core == odd(offset)
                tile = pl.ds(pl.multiple_of((chip ^ offset) * 2 * own, 2 * own), 2 * own)

                def joined(ref):
                    a, b = ref[mine], ref[theirs]
                    return jnp.where(
                        first, jnp.concatenate([a, b], 0), jnp.concatenate([b, a], 0)
                    )

                turned = joined(rot)
                value = 0.95 * second[tile] + 0.05 * turned * turned
                second_next[tile] = value
                ratio = joined(mom) / (jnp.sqrt(value) + 1e-08)
                rot[mine] = jnp.where(first, ratio[:own], ratio[own:])
                rot[theirs] = jnp.where(first, ratio[own:], ratio[:own])

    scaled[...] = rot[...].astype(jnp.bfloat16)


def scaled_rotation(orders, own, basis, grad, moment, rot_half, second):
    count, rows = basis.shape[0], grad.shape[1]
    return pl.pallas_call(
        functools.partial(scale_kernel, orders, own),
        in_specs=[INSIDE] * 5,
        out_specs=[INSIDE] * 2,
        out_shape=[
            pltpu.VMEM((count, rows), jnp.bfloat16),
            jax.ShapeDtypeStruct((count, rows), jnp.float32),
        ],
        scratch_shapes=[pltpu.VMEM((count, rows), jnp.float32)] * 2,
        compiler_params=PARAMS,
        name="scale",
    )(*map(inside, (basis, grad, moment, rot_half, second)))


def update_kernel(basis, scaled, out, held, sems):
    copies = []
    for i, (at, size) in enumerate(cuts(out.shape[0], 640)):
        part = pl.ds(at, size)
        held[part] = dot(basis[:, part], scaled[...], ((0,), (0,))).astype(jnp.bfloat16)
        copy = pltpu.make_async_copy(held.at[part], out.at[part], sems.at[i])
        copy.start()
        copies.append(copy)
    for copy in copies:
        copy.wait()


def new_update(basis, scaled):
    depth, rows = basis.shape[1], scaled.shape[1]
    return pl.pallas_call(
        update_kernel,
        in_specs=[INSIDE] * 2,
        out_specs=ANYWHERE,
        out_shape=jax.ShapeDtypeStruct((depth, rows), jnp.bfloat16),
        scratch_shapes=[
            pltpu.VMEM((depth, rows), jnp.bfloat16),
            pltpu.SemaphoreType.DMA((len(cuts(depth, 640)),)),
        ],
        compiler_params=PARAMS,
        name="update",
    )(inside(basis), inside(scaled))


def shards(n, grad, moment, second, basis):
    bits = n.bit_length() - 2
    own = basis.shape[0]
    far, near = (bits - 1,), tuple(reversed(range(bits - 1)))
    orders = (far + near[-1:] + near[:-1], far + near)

    def exchange(value, step):
        pairs = [(i, i ^ (2 << orders[odd(i)][step]) ^ 1) for i in range(n)]
        return lax.ppermute(value, "rows", pairs)

    def across(value):
        return lax.ppermute(value, "rows", [(i, i ^ 1) for i in range(n)])

    grad, moment, second = grad.T, moment.T, second.T

    come = exchange(basis, 0)
    grad, held = load(grad, basis)
    come, grad, held = tie(come, grad, held)
    other = across(grad)
    held = jnp.concatenate([held, come], 0)
    for step in range(1, bits - 2):
        held = jnp.concatenate([held, exchange(held, step)], 0)
    first = exchange(held, bits - 2)
    second_hand = exchange(held, bits - 1)
    first, grad = tie(first, grad)
    last = exchange(first, bits - 1)
    second_hand, grad, other = tie(second_hand, grad, other)
    grad_rows, other_rows = transposed(grad, other)
    last, grad_rows, other_rows = tie(last, grad_rows, other_rows)
    held, rot_half, kept, sent = power_products(
        (held, first, second_hand, last), (grad, other, grad_rows, other_rows)
    )
    come = exchange(sent, bits - 1)
    moment, _ = tie(moment, sent)
    theirs = across(held)
    moment_in, moment_next = new_moment(grad, moment)
    come, moment_in, moment_next = tie(come, moment_in, moment_next)
    for step in reversed(range(bits)):
        if step == 0:
            break
        kept = kept + come.astype(jnp.float32)
        half = kept.shape[0] // 2
        come = exchange(kept[half:].astype(jnp.bfloat16), step - 1)
        kept = kept[:half]
        if step == bits - 1:
            theirs, kept = tie(theirs, kept)
            whole = jnp.concatenate([held, theirs], 0)
            scaled, second_next = scaled_rotation(
                orders, own, whole, grad, moment_in, rot_half, second
            )
            come, scaled, second_next = tie(come, scaled, second_next)
        if step == bits - 2:
            scaled, kept = tie(scaled, kept)
            update = new_update(whole, scaled)
            come, update = tie(come, update)
    basis_next = normalised(kept, come)
    return update.T, moment_next.T, second_next.T, basis_next


def solution(mesh):
    n = mesh.shape["rows"]
    placed = P(("groups", "rows"), None)
    return jax.shard_map(
        lambda *arrays: shards(n, *arrays),
        mesh=mesh,
        in_specs=(placed,) * 4,
        out_specs=(placed,) * 4,
        check_vma=False,
    )
```
